512 devices in a mesh: dp: 32 (over x_lo, y, core), bfly: 16 (over z, x_hi).
Axes of the slice: x: 4 (x_hi: 2, x_lo: 2; x = x_hi * 2 + x_lo), y: 8, z: 8, core: 2. Of those that a mesh axis runs over, the one named last changes fastest.
Arguments:
- tokens: bfloat16 [8192, 16384], P('dp', 'bfly'), may hold values from -6 to 6
- weight_a: bfloat16 [2, 64, 256, 256], P(None, 'bfly'), may hold values from -0.25 to 0.25
- weight_b: bfloat16 [2, 64, 256, 256], P(None, 'bfly'), may hold values from -0.25 to 0.25
- upstream: bfloat16 [8192, 16384], P('dp', 'bfly'), may hold values from -6 to 6
Outputs:
- output: bfloat16 [8192, 16384], P('dp', 'bfly')
- grad_input: bfloat16 [8192, 16384], P('dp', 'bfly')
- grad_weight_a: float32 [256, 2, 64, 256], P('dp', None, 'bfly')
- grad_weight_b: float32 [256, 2, 64, 256], P('dp', None, 'bfly')
The draws below stay inside these ranges and needn't reach their ends.
All inputs are finite; a program needn't handle non-finite values.
Results may differ from the reference program's by a relative error of at most 0.005.
Values may be sent and summed in bfloat16 or wider, within the bound.
A program may use at most 64 MiB of HBM per device.

```python
import jax
import jax.numpy as jnp
import numpy as np

D = 16384
BS = 256
BLOCKS = 64
BLK_DEV = 4
TOKENS = 8192


def level_of(stream_key, dims, split, smallest, top_value):
    gain, own = 1.0, jax.random.fold_in(stream_key, 6)
    for position, shards_of in split:
        heights = jnp.exp(jax.random.uniform(jax.random.fold_in(own, position), (shards_of,), jnp.float32, smallest / len(split), top_value / len(split)))
        gain = gain * jnp.repeat(heights, dims[position] // shards_of).reshape([-1 if axis == position else 1 for axis in range(len(dims))])
    return gain


def centred(rng, shape, scale, bound, pieces=(), held_as=jnp.bfloat16):
    gain = level_of(rng, shape, pieces, -0.22, 0.18) if pieces else 1.0
    values = jax.random.normal(rng, shape, jnp.float32) * scale * gain
    return jnp.minimum(jnp.maximum(values, -bound), bound).astype(held_as)


def setup_inputs(seed: int = 0) -> dict:
    streams_of = jax.random.split(jax.random.key(seed), 5)
    tokens = centred(streams_of[0], (TOKENS, D), 1.0, 6.0, ((0, 32), (1, 16)))
    weight_a = centred(streams_of[1], (2, BLOCKS, BS, BS), (2 * BS) ** -0.5, 0.25, ((1, 16),))
    weight_b = centred(streams_of[2], (2, BLOCKS, BS, BS), (2 * BS) ** -0.5, 0.25, ((1, 16),))
    upstream = centred(streams_of[3], (TOKENS, D), 1.0, 6.0, ((0, 32), (1, 16)))
    return dict(tokens=tokens, weight_a=weight_a, weight_b=weight_b, upstream=upstream)


def activate(values):
    return jax.nn.gelu(values, approximate=False)

def reference(tokens, weight_a, weight_b, upstream):
    tok_rows = tokens.shape[0]
    part_a = np.arange(BLOCKS) ^ BLOCKS // 2
    part_b = np.arange(BLOCKS) ^ BLK_DEV
    inputs = tokens.reshape(tok_rows, BLOCKS, BS).astype(jnp.float32)
    grads_out = upstream.reshape(tok_rows, BLOCKS, BS).astype(jnp.float32)
    wa_f = weight_a.astype(jnp.float32)
    wb_f = weight_b.astype(jnp.float32)
    pre_act = jnp.einsum('tir,irc->tic', inputs, wa_f[0]) + jnp.einsum('tir,irc->tic', inputs[:, part_a], wa_f[1])
    hidden = activate(pre_act).astype(jnp.bfloat16)
    hidden_f = hidden.astype(jnp.float32)
    result = jnp.einsum('tir,irc->tic', hidden_f, wb_f[0]) + jnp.einsum('tir,irc->tic', hidden_f[:, part_b], wb_f[1])
    output = result.astype(jnp.bfloat16).reshape(tok_rows, D)
    grad_hidden = jnp.einsum('tic,irc->tir', grads_out, wb_f[0]) + jnp.einsum('tic,irc->tir', grads_out[:, part_b], wb_f[1][part_b])
    pull = jax.vjp(activate, pre_act)[1]
    grad_pre = pull(grad_hidden)[0].astype(jnp.bfloat16)
    grad_pre_f = grad_pre.astype(jnp.float32)
    grad_in = jnp.einsum('tic,irc->tir', grad_pre_f, wa_f[0]) + jnp.einsum('tic,irc->tir', grad_pre_f[:, part_a], wa_f[1][part_a])
    grad_input = grad_in.astype(jnp.bfloat16).reshape(tok_rows, D)
    norm_scale = jnp.float32(TOKENS) ** (-0.5)
    grad_b = jnp.stack([jnp.einsum('tir,tic->ric', hidden_f, grads_out), jnp.einsum('tir,tic->ric', hidden_f[:, part_b], grads_out)], 1) * norm_scale
    grad_a = jnp.stack([jnp.einsum('tir,tic->ric', inputs, grad_pre_f), jnp.einsum('tir,tic->ric', inputs[:, part_a], grad_pre_f)], 1) * norm_scale
    return (output, grad_input, grad_a, grad_b)
```

```python
import functools

import jax
import jax.numpy as jnp
from jax import lax
from jax.experimental import pallas as pl
from jax.experimental.pallas import tpu as pltpu
from jax.sharding import PartitionSpec as P

MESH = pl.DeviceIdType.MESH
NY = 8
NZ = 8
F32 = jnp.float32
BF16 = jnp.bfloat16
ROWS = 32


def dot_nn(a, b):
    return lax.dot_general(a, b, (((1,), (0,)), ((), ())), preferred_element_type=F32)


def dot_nt(a, b):
    return lax.dot_general(a, b, (((1,), (1,)), ((), ())), preferred_element_type=F32)


def dot_tn(a, b):
    return lax.dot_general(a, b, (((0,), (0,)), ((), ())), preferred_element_type=F32)


def main_kernel(
    scale,
    x_hbm,
    g_hbm,
    wa_hbm,
    wb_hbm,
    out_hbm,
    gi_hbm,
    ga_hbm,
    gb_hbm,
    xv,
    gv,
    wav,
    wbv,
    xp,
    ps,
    pr,
    hv,
    hp,
    cs,
    cr,
    uf,
    dhf,
    du,
    own,
    loc,
    sib,
    ysend,
    yrecv,
    tsum,
    trecv,
    outv,
    giv,
    gav,
    gbv,
    load_sem,
    store_sem,
    x_ss,
    x_rs,
    p_ss,
    p_rs,
    h_ss,
    h_rs,
    c_ss,
    c_rs,
    m_ss,
    m_rs,
    y_ss,
    y_rs,
    t_ss,
    t_rs,
):
    n_blk, size = xv.shape[0], xv.shape[1]
    dp, bfly = lax.axis_index("dp"), lax.axis_index("bfly")
    core, y, xl = dp % 2, (dp // 2) % NY, dp // (2 * NY)
    z, xh = bfly // 2, bfly % 2
    z_dev = (dp, ((z + NZ // 2) % NZ) * 2 + xh)
    xh_dev = (dp, z * 2 + (1 - xh))
    core_dev = (dp + 1 - 2 * core, bfly)
    xl_dev = (((1 - xl) * NY + y) * 2 + core, bfly)

    def y_dev(to):
        return ((xl * NY + to) * 2 + core, bfly)

    def remote(src, dst, ss, rs, dev):
        return pltpu.make_async_remote_copy(
            src_ref=src, dst_ref=dst, send_sem=ss, recv_sem=rs, device_id=dev, device_id_type=MESH
        )

    def cols(k):
        return pl.ds(k * size, size)

    load_g = [pltpu.make_async_copy(g_hbm.at[:, cols(k)], gv.at[k], load_sem.at[k]) for k in range(n_blk)]
    load_x = [
        pltpu.make_async_copy(x_hbm.at[:, cols(k)], xv.at[k], load_sem.at[n_blk + k]) for k in range(n_blk)
    ]
    load_wb = [pltpu.make_async_copy(wb_hbm.at[s], wbv.at[s], load_sem.at[2 * n_blk + s]) for s in range(2)]
    load_wa = [pltpu.make_async_copy(wa_hbm.at[s], wav.at[s], load_sem.at[2 * n_blk + 2 + s]) for s in range(2)]
    load_wb[1].start()
    for c in load_g:
        c.start()
    for c in load_x:
        c.start()
    load_wa[0].start()
    load_wb[0].start()
    load_wa[1].start()

    barrier = pltpu.get_barrier_semaphore()
    for dev in [z_dev, xh_dev, core_dev, xl_dev] + [y_dev((y + j) % NY) for j in range(1, NY)]:
        pl.semaphore_signal(barrier, inc=1, device_id=dev, device_id_type=MESH)

    load_wb[1].wait()
    for k in range(n_blk):
        load_g[k].wait()
        ps[k] = dot_nt(gv[k], wbv[1, k]).astype(BF16)

    pl.semaphore_wait(barrier, 3 + NY)

    send_x = [remote(x_hbm.at[:, cols(k)], xp.at[k], x_ss.at[k], x_rs.at[k], z_dev) for k in range(n_blk)]
    send_p = [remote(ps.at[k], pr.at[k], p_ss.at[k], p_rs.at[k], xh_dev) for k in range(n_blk)]
    for c in send_x:
        c.start()
    for c in send_p:
        c.start()
    send_h = [remote(hv.at[k], hp.at[k], h_ss.at[k], h_rs.at[k], xh_dev) for k in range(n_blk)]
    send_c = [remote(cs.at[k], cr.at[k], c_ss.at[k], c_rs.at[k], z_dev) for k in range(n_blk)]
    send_m = [
        [
            remote(
                loc.at[k, pl.ds(2 * h, 2), :, :, 1 - core],
                sib.at[k, pl.ds(2 * h, 2)],
                m_ss.at[k, h],
                m_rs.at[k, h],
                core_dev,
            )
            for h in range(2)
        ]
        for k in range(n_blk)
    ]
    send_y = [
        [
            remote(
                ysend.at[k, (y + j) % NY],
                yrecv.at[k, j - 1],
                y_ss.at[k, j - 1],
                y_rs.at[k, j - 1],
                y_dev((y + j) % NY),
            )
            for j in range(1, NY)
        ]
        for k in range(n_blk)
    ]
    send_t = [remote(tsum.at[k, 1 - xl], trecv.at[k], t_ss.at[k], t_rs.at[k], xl_dev) for k in range(n_blk)]
    store_out = [
        pltpu.make_async_copy(outv.at[k], out_hbm.at[:, cols(k)], store_sem.at[k]) for k in range(n_blk)
    ]
    store_gi = [
        pltpu.make_async_copy(giv.at[k], gi_hbm.at[:, cols(k)], store_sem.at[n_blk + k]) for k in range(n_blk)
    ]
    store_ga = pltpu.make_async_copy(gav, ga_hbm, store_sem.at[2 * n_blk])
    store_gb = pltpu.make_async_copy(gbv, gb_hbm, store_sem.at[2 * n_blk + 1])

    def keep(k, m, value):
        loc[k, m] = value.reshape(loc.shape[2:])

    def first_factor(k):
        load_x[k].wait()
        if k == 0:
            load_wa[0].wait()
            load_wa[1].wait()
            load_wb[0].wait()
        dhf[...] = dot_nt(gv[k], wbv[0, k])
        uf[...] = dot_nn(xv[k], wav[0, k])
        send_x[k].wait_recv()
        uf[...] += dot_nn(xp[k], wav[1, k])
        send_p[k].wait_recv()

        def rows(i, _):
            at = pl.ds(pl.multiple_of(i * ROWS, ROWS), ROWS)
            u = uf[at, :]
            dh = dhf[at, :] + pr[k, at, :].astype(F32)
            phi = 0.5 + 0.5 * lax.erf(u * F32(0.5**0.5))
            dens = jnp.exp(u * u * F32(-0.5)) * F32(0.3989422804014327)
            hv[k, at, :] = (u * phi).astype(BF16)
            du[k, at, :] = (dh * (phi + u * dens)).astype(BF16)
            return 0

        lax.fori_loop(0, size // ROWS, rows, 0)
        send_h[k].start()
        cs[k] = dot_nt(du[k], wav[1, k]).astype(BF16)
        send_c[k].start()
        keep(k, 0, dot_tn(xv[k], du[k]))
        keep(k, 1, dot_tn(xp[k], du[k]))
        send_m[k][0].start()
        own[k] = dot_nt(du[k], wav[0, k])

    def second_factor(k):
        keep(k, 2, dot_tn(hv[k], gv[k]))
        mine = dot_nn(hv[k], wbv[0, k])
        send_h[k].wait_recv()
        keep(k, 3, dot_tn(hp[k], gv[k]))
        send_m[k][1].start()
        outv[k] = (mine + dot_nn(hp[k], wbv[1, k])).astype(BF16)
        store_out[k].start()

    def to_owners(k):
        for h in range(2):
            send_m[k][h].wait_recv()
        for m in range(4):
            both = [loc[k, m, s, :, core] + sib[k, m, s] for s in range(2)]
            ysend[k, :, m] = jnp.concatenate(both, axis=1).astype(BF16)
        for j in (4, 3, 5, 2, 6, 1, 7):
            send_y[k][j - 1].start()

    def sum_y(k):
        for j in range(1, NY):
            send_y[k][j - 1].wait_recv()
        for m in range(4):
            mine = [loc[k, m, s, y, core] + sib[k, m, s, y] for s in range(2)]
            total = jnp.concatenate(mine, axis=0)
            for j in range(NY - 1):
                total = total + yrecv[k, j, m].astype(F32)
            tsum[k, 0, m] = total[:8]
            tsum[k, 1, m] = total[8:]
        send_t[k].start()

    def finish_weights(k):
        send_t[k].wait_recv()
        for m in range(4):
            value = (tsum[k, xl, m] + trecv[k, m]) * scale
            into = gav if m < 2 else gbv
            for r in range(8):
                into[r, m % 2, pl.ds(k, 1), :] = value[r : r + 1, :]

    def finish_input(k):
        send_c[k].wait_recv()
        giv[k] = (own[k] + cr[k].astype(F32)).astype(BF16)
        store_gi[k].start()

    first_factor(0)
    first_factor(1)
    second_factor(0)
    first_factor(2)
    second_factor(1)
    to_owners(0)
    first_factor(3)
    second_factor(2)
    to_owners(1)
    sum_y(0)
    second_factor(3)
    to_owners(2)
    sum_y(1)
    finish_weights(0)
    to_owners(3)
    sum_y(2)
    finish_weights(1)
    finish_input(0)
    sum_y(3)
    finish_weights(2)
    finish_input(1)
    finish_weights(3)
    store_ga.start()
    store_gb.start()
    finish_input(2)
    for k in range(n_blk):
        for c in [send_x[k], send_p[k], send_h[k], *send_m[k], *send_y[k], send_t[k]]:
            c.wait_send()
        store_out[k].wait()
    store_ga.wait()
    store_gb.wait()
    finish_input(3)
    for k in range(n_blk):
        send_c[k].wait_send()
        store_gi[k].wait()


def copy_kernel(*refs):
    n = len(refs) // 2
    sems = refs[-1]
    copies = [pltpu.make_async_copy(refs[i], refs[n + i], sems.at[i]) for i in range(n)]
    for c in copies:
        c.start()
    for c in copies:
        c.wait()


def shards(n_dp, tokens, weight_a, weight_b, upstream):
    rows, width = tokens.shape
    n_blk, size = weight_a.shape[1], weight_a.shape[2]
    own_rows = size // n_dp
    scale = float((rows * n_dp) ** -0.5)
    results = (
        jax.ShapeDtypeStruct((rows, width), BF16),
        jax.ShapeDtypeStruct((rows, width), BF16),
        jax.ShapeDtypeStruct((own_rows, 2, n_blk, size), F32),
        jax.ShapeDtypeStruct((own_rows, 2, n_blk, size), F32),
    )
    anywhere = pl.BlockSpec(memory_space=pl.ANY)
    act = pltpu.VMEM((n_blk, rows, size), BF16)
    weights = pltpu.VMEM((2, n_blk, size, size), BF16)
    dma = pltpu.SemaphoreType.DMA
    made = pl.pallas_call(
        functools.partial(main_kernel, scale),
        out_shape=results,
        in_specs=[anywhere] * 4,
        out_specs=[anywhere] * 4,
        scratch_shapes=[
            act,
            act,
            weights,
            weights,
            act,
            act,
            act,
            act,
            act,
            act,
            act,
            pltpu.VMEM((rows, size), F32),
            pltpu.VMEM((rows, size), F32),
            act,
            pltpu.VMEM((n_blk, rows, size), F32),
            pltpu.VMEM((n_blk, 4, 2, NY, 2, own_rows, size), F32),
            pltpu.VMEM((n_blk, 4, 2, NY, own_rows, size), F32),
            pltpu.VMEM((n_blk, NY, 4, 2 * own_rows, size), BF16),
            pltpu.VMEM((n_blk, NY - 1, 4, 2 * own_rows, size), BF16),
            pltpu.VMEM((n_blk, 2, 4, own_rows, size), F32),
            pltpu.VMEM((n_blk, 4, own_rows, size), F32),
            act,
            act,
            pltpu.VMEM((own_rows, 2, n_blk, size), F32),
            pltpu.VMEM((own_rows, 2, n_blk, size), F32),
            dma((2 * n_blk + 4,)),
            dma((2 * n_blk + 2,)),
            dma((n_blk,)),
            dma((n_blk,)),
            dma((n_blk,)),
            dma((n_blk,)),
            dma((n_blk,)),
            dma((n_blk,)),
            dma((n_blk,)),
            dma((n_blk,)),
            dma((n_blk, 2)),
            dma((n_blk, 2)),
            dma((n_blk, NY - 1)),
            dma((n_blk, NY - 1)),
            dma((n_blk,)),
            dma((n_blk,)),
        ],
        compiler_params=pltpu.CompilerParams(
            collective_id=0, has_side_effects=True, vmem_limit_bytes=48 << 20
        ),
    )(tokens, upstream, weight_a, weight_b)
    return pl.pallas_call(
        copy_kernel,
        out_shape=results,
        in_specs=[anywhere] * 4,
        out_specs=[anywhere] * 4,
        scratch_shapes=[dma((4,))],
    )(*made)


def solution(mesh):
    in_specs = (
        P("dp", "bfly"),
        P(None, "bfly", None, None),
        P(None, "bfly", None, None),
        P("dp", "bfly"),
    )
    out_specs = (
        P("dp", "bfly"),
        P("dp", "bfly"),
        P("dp", None, "bfly", None),
        P("dp", None, "bfly", None),
    )
    return jax.shard_map(
        functools.partial(shards, mesh.shape["dp"]),
        mesh=mesh,
        in_specs=in_specs,
        out_specs=out_specs,
        check_vma=False,
    )
```

```python
import functools

import jax
import jax.numpy as jnp
from jax import lax
from jax.experimental import pallas as pl
from jax.experimental.pallas import tpu as pltpu
from jax.sharding import PartitionSpec as P

MESH = pl.DeviceIdType.MESH
NY = 8
NZ = 8
F32 = jnp.float32
BF16 = jnp.bfloat16
SIGNAL_AT = 2
ROWS = 32


def dot_nn(a, b):
    return lax.dot_general(a, b, (((1,), (0,)), ((), ())), preferred_element_type=F32)


def dot_nt(a, b):
    return lax.dot_general(a, b, (((1,), (1,)), ((), ())), preferred_element_type=F32)


def dot_tn(a, b):
    return lax.dot_general(a, b, (((0,), (0,)), ((), ())), preferred_element_type=F32)


def main_kernel(
    scale,
    x_hbm,
    g_hbm,
    wa_hbm,
    wb_hbm,
    out_hbm,
    gi_hbm,
    ga_hbm,
    gb_hbm,
    xv,
    gv,
    wav,
    wbv,
    xp,
    ps,
    pr,
    hv,
    hp,
    cs,
    cr,
    uf,
    dhf,
    du,
    own,
    loc,
    sib,
    ysend,
    yrecv,
    tsum,
    trecv,
    outv,
    giv,
    gav,
    gbv,
    load_sem,
    store_sem,
    x_ss,
    x_rs,
    p_ss,
    p_rs,
    h_ss,
    h_rs,
    c_ss,
    c_rs,
    m_ss,
    m_rs,
    y_ss,
    y_rs,
    t_ss,
    t_rs,
    phase,
):
    n_blk, size = xv.shape[0], xv.shape[1]
    dp, bfly = lax.axis_index("dp"), lax.axis_index("bfly")
    core, y, xl = dp % 2, (dp // 2) % NY, dp // (2 * NY)
    z, xh = bfly // 2, bfly % 2
    z_dev = (dp, ((z + NZ // 2) % NZ) * 2 + xh)
    xh_dev = (dp, z * 2 + (1 - xh))
    core_dev = (dp + 1 - 2 * core, bfly)
    xl_dev = (((1 - xl) * NY + y) * 2 + core, bfly)

    ring = [(dp, ((z + j) % NZ) * 2 + xh) for j in range(1, NZ)]

    def y_dev(to):
        return ((xl * NY + to) * 2 + core, bfly)

    def remote(src, dst, ss, rs, dev):
        return pltpu.make_async_remote_copy(
            src_ref=src, dst_ref=dst, send_sem=ss, recv_sem=rs, device_id=dev, device_id_type=MESH
        )

    def cols(k):
        return pl.ds(k * size, size)

    load_g = [pltpu.make_async_copy(g_hbm.at[:, cols(k)], gv.at[k], load_sem.at[k]) for k in range(n_blk)]
    load_x = [
        pltpu.make_async_copy(x_hbm.at[:, cols(k)], xv.at[k], load_sem.at[n_blk + k]) for k in range(n_blk)
    ]
    load_wb = [pltpu.make_async_copy(wb_hbm.at[s], wbv.at[s], load_sem.at[2 * n_blk + s]) for s in range(2)]
    load_wa = [pltpu.make_async_copy(wa_hbm.at[s], wav.at[s], load_sem.at[2 * n_blk + 2 + s]) for s in range(2)]
    load_wb[1].start()
    for c in load_g:
        c.start()
    for c in load_x:
        c.start()
    load_wa[0].start()
    load_wb[0].start()
    load_wa[1].start()

    barrier = pltpu.get_barrier_semaphore()
    for dev in [xh_dev, core_dev, xl_dev] + ring + [y_dev((y + j) % NY) for j in range(1, NY)]:
        pl.semaphore_signal(barrier, inc=1, device_id=dev, device_id_type=MESH)

    load_wb[1].wait()
    for k in range(n_blk):
        load_g[k].wait()
        ps[k] = dot_nt(gv[k], wbv[1, k]).astype(BF16)

    pl.semaphore_wait(barrier, 1 + NY + NZ)

    send_x = [remote(x_hbm.at[:, cols(k)], xp.at[k], x_ss.at[k], x_rs.at[k], z_dev) for k in range(n_blk)]
    send_p = [remote(ps.at[k], pr.at[k], p_ss.at[k], p_rs.at[k], xh_dev) for k in range(n_blk)]
    for c in send_x:
        c.start()
    for c in send_p:
        c.start()
    send_h = [remote(hv.at[k], hp.at[k], h_ss.at[k], h_rs.at[k], xh_dev) for k in range(n_blk)]
    send_c = [remote(cs.at[k], cr.at[k], c_ss.at[k], c_rs.at[k], z_dev) for k in range(n_blk)]
    send_m = [
        [
            remote(
                loc.at[k, pl.ds(2 * h, 2), :, :, 1 - core],
                sib.at[k, pl.ds(2 * h, 2)],
                m_ss.at[k, h],
                m_rs.at[k, h],
                core_dev,
            )
            for h in range(2)
        ]
        for k in range(n_blk)
    ]
    send_y = [
        [
            remote(
                ysend.at[k, (y + j) % NY],
                yrecv.at[k, j - 1],
                y_ss.at[k, j - 1],
                y_rs.at[k, j - 1],
                y_dev((y + j) % NY),
            )
            for j in range(1, NY)
        ]
        for k in range(n_blk)
    ]
    send_t = [remote(tsum.at[k, 1 - xl], trecv.at[k], t_ss.at[k], t_rs.at[k], xl_dev) for k in range(n_blk)]
    store_out = [
        pltpu.make_async_copy(outv.at[k], out_hbm.at[:, cols(k)], store_sem.at[k]) for k in range(n_blk)
    ]
    store_gi = [
        pltpu.make_async_copy(giv.at[k], gi_hbm.at[:, cols(k)], store_sem.at[n_blk + k]) for k in range(n_blk)
    ]
    store_ga = pltpu.make_async_copy(gav, ga_hbm, store_sem.at[2 * n_blk])
    store_gb = pltpu.make_async_copy(gbv, gb_hbm, store_sem.at[2 * n_blk + 1])

    def keep(k, m, value):
        loc[k, m] = value.reshape(loc.shape[2:])

    def first_factor(k):
        load_x[k].wait()
        if k == 0:
            load_wa[0].wait()
            load_wa[1].wait()
            load_wb[0].wait()
        dhf[...] = dot_nt(gv[k], wbv[0, k])
        uf[...] = dot_nn(xv[k], wav[0, k])
        send_x[k].wait_recv()
        if k == SIGNAL_AT:
            for dev in ring:
                pl.semaphore_signal(phase, inc=1, device_id=dev, device_id_type=MESH)
        uf[...] += dot_nn(xp[k], wav[1, k])
        send_p[k].wait_recv()

        def rows(i, _):
            at = pl.ds(pl.multiple_of(i * ROWS, ROWS), ROWS)
            u = uf[at, :]
            dh = dhf[at, :] + pr[k, at, :].astype(F32)
            phi = 0.5 + 0.5 * lax.erf(u * F32(0.5**0.5))
            dens = jnp.exp(u * u * F32(-0.5)) * F32(0.3989422804014327)
            hv[k, at, :] = (u * phi).astype(BF16)
            du[k, at, :] = (dh * (phi + u * dens)).astype(BF16)
            return 0

        lax.fori_loop(0, size // ROWS, rows, 0)
        send_h[k].start()
        cs[k] = dot_nt(du[k], wav[1, k]).astype(BF16)
        keep(k, 0, dot_tn(xv[k], du[k]))
        keep(k, 1, dot_tn(xp[k], du[k]))
        send_m[k][0].start()
        own[k] = dot_nt(du[k], wav[0, k])

    def second_factor(k):
        keep(k, 2, dot_tn(hv[k], gv[k]))
        mine = dot_nn(hv[k], wbv[0, k])
        send_h[k].wait_recv()
        keep(k, 3, dot_tn(hp[k], gv[k]))
        send_m[k][1].start()
        outv[k] = (mine + dot_nn(hp[k], wbv[1, k])).astype(BF16)
        store_out[k].start()

    def to_owners(k):
        for h in range(2):
            send_m[k][h].wait_recv()
        for m in range(4):
            both = [loc[k, m, s, :, core] + sib[k, m, s] for s in range(2)]
            ysend[k, :, m] = jnp.concatenate(both, axis=1).astype(BF16)
        for j in (4, 3, 5, 2, 6, 1, 7):
            send_y[k][j - 1].start()

    def sum_y(k):
        for j in range(1, NY):
            send_y[k][j - 1].wait_recv()
        for m in range(4):
            mine = [loc[k, m, s, y, core] + sib[k, m, s, y] for s in range(2)]
            total = jnp.concatenate(mine, axis=0)
            for j in range(NY - 1):
                total = total + yrecv[k, j, m].astype(F32)
            tsum[k, 0, m] = total[:8]
            tsum[k, 1, m] = total[8:]
        send_t[k].start()

    def finish_weights(k):
        send_t[k].wait_recv()
        for m in range(4):
            value = (tsum[k, xl, m] + trecv[k, m]) * scale
            into = gav if m < 2 else gbv
            for r in range(8):
                into[r, m % 2, pl.ds(k, 1), :] = value[r : r + 1, :]

    def finish_input(k):
        send_c[k].wait_recv()
        giv[k] = (own[k] + cr[k].astype(F32)).astype(BF16)
        store_gi[k].start()

    first_factor(0)
    first_factor(1)
    second_factor(0)
    first_factor(2)
    second_factor(1)
    to_owners(0)
    first_factor(3)
    second_factor(2)
    to_owners(1)
    pl.semaphore_wait(phase, NZ - 1)
    for c in send_c:
        c.start()
    sum_y(0)
    second_factor(3)
    to_owners(2)
    sum_y(1)
    finish_weights(0)
    to_owners(3)
    sum_y(2)
    finish_weights(1)
    finish_input(0)
    sum_y(3)
    finish_weights(2)
    finish_input(1)
    finish_weights(3)
    store_ga.start()
    store_gb.start()
    finish_input(2)
    for k in range(n_blk):
        for c in [send_x[k], send_p[k], send_h[k], *send_m[k], *send_y[k], send_t[k]]:
            c.wait_send()
        store_out[k].wait()
    store_ga.wait()
    store_gb.wait()
    finish_input(3)
    for k in range(n_blk):
        send_c[k].wait_send()
        store_gi[k].wait()


def shards(n_dp, tokens, weight_a, weight_b, upstream):
    rows, width = tokens.shape
    n_blk, size = weight_a.shape[1], weight_a.shape[2]
    own_rows = size // n_dp
    scale = float((rows * n_dp) ** -0.5)
    results = (
        jax.ShapeDtypeStruct((rows, width), BF16),
        jax.ShapeDtypeStruct((rows, width), BF16),
        jax.ShapeDtypeStruct((own_rows, 2, n_blk, size), F32),
        jax.ShapeDtypeStruct((own_rows, 2, n_blk, size), F32),
    )
    anywhere = pl.BlockSpec(memory_space=pl.ANY)
    act = pltpu.VMEM((n_blk, rows, size), BF16)
    weights = pltpu.VMEM((2, n_blk, size, size), BF16)
    dma = pltpu.SemaphoreType.DMA
    made = pl.pallas_call(
        functools.partial(main_kernel, scale),
        out_shape=results,
        in_specs=[anywhere] * 4,
        out_specs=[anywhere] * 4,
        scratch_shapes=[
            act,
            act,
            weights,
            weights,
            act,
            act,
            act,
            act,
            act,
            act,
            act,
            pltpu.VMEM((rows, size), F32),
            pltpu.VMEM((rows, size), F32),
            act,
            pltpu.VMEM((n_blk, rows, size), F32),
            pltpu.VMEM((n_blk, 4, 2, NY, 2, own_rows, size), F32),
            pltpu.VMEM((n_blk, 4, 2, NY, own_rows, size), F32),
            pltpu.VMEM((n_blk, NY, 4, 2 * own_rows, size), BF16),
            pltpu.VMEM((n_blk, NY - 1, 4, 2 * own_rows, size), BF16),
            pltpu.VMEM((n_blk, 2, 4, own_rows, size), F32),
            pltpu.VMEM((n_blk, 4, own_rows, size), F32),
            act,
            act,
            pltpu.VMEM((own_rows, 2, n_blk, size), F32),
            pltpu.VMEM((own_rows, 2, n_blk, size), F32),
            dma((2 * n_blk + 4,)),
            dma((2 * n_blk + 2,)),
            dma((n_blk,)),
            dma((n_blk,)),
            dma((n_blk,)),
            dma((n_blk,)),
            dma((n_blk,)),
            dma((n_blk,)),
            dma((n_blk,)),
            dma((n_blk,)),
            dma((n_blk, 2)),
            dma((n_blk, 2)),
            dma((n_blk, NY - 1)),
            dma((n_blk, NY - 1)),
            dma((n_blk,)),
            dma((n_blk,)),
            pltpu.SemaphoreType.REGULAR,
        ],
        compiler_params=pltpu.CompilerParams(
            collective_id=0, has_side_effects=True, vmem_limit_bytes=60 << 20
        ),
    )(tokens, upstream, weight_a, weight_b)
    vm = pl.BlockSpec(memory_space=pltpu.VMEM)
    return pl.pallas_call(
        copy_kernel,
        out_shape=results,
        in_specs=[vm] * 4,
        out_specs=[vm] * 4,
    )(*made)


def copy_kernel(*refs):
    for i in range(4):
        refs[4 + i][...] = refs[i][...]


def solution(mesh):
    in_specs = (
        P("dp", "bfly"),
        P(None, "bfly", None, None),
        P(None, "bfly", None, None),
        P("dp", "bfly"),
    )
    out_specs = (
        P("dp", "bfly"),
        P("dp", "bfly"),
        P("dp", None, "bfly", None),
        P("dp", None, "bfly", None),
    )
    return jax.shard_map(
        functools.partial(shards, mesh.shape["dp"]),
        mesh=mesh,
        in_specs=in_specs,
        out_specs=out_specs,
        check_vma=False,
    )
```

```python
import functools

import jax
import jax.numpy as jnp
from jax import lax
from jax.experimental import pallas as pl
from jax.experimental.pallas import tpu as pltpu
from jax.sharding import PartitionSpec as P

MESH = pl.DeviceIdType.MESH
NY = 8
NZ = 8
F32 = jnp.float32
BF16 = jnp.bfloat16
SIGNAL_AT = 2
ROWS = 32


def dot_nn(a, b):
    return lax.dot_general(a, b, (((1,), (0,)), ((), ())), preferred_element_type=F32)


def dot_nt(a, b):
    return lax.dot_general(a, b, (((1,), (1,)), ((), ())), preferred_element_type=F32)


def dot_tn(a, b):
    return lax.dot_general(a, b, (((0,), (0,)), ((), ())), preferred_element_type=F32)


def main_kernel(
    scale,
    x_hbm,
    g_hbm,
    wa_hbm,
    wb_hbm,
    out_hbm,
    gi_hbm,
    ga_hbm,
    gb_hbm,
    own_hbm,
    last_hbm,
    xv,
    gv,
    wav,
    wbv,
    xp,
    ps,
    pr,
    hv,
    hp,
    cs,
    cr,
    uf,
    dhf,
    du,
    own,
    loc,
    sib,
    ysend,
    yrecv,
    tsum,
    trecv,
    outv,
    giv,
    gav,
    gbv,
    load_sem,
    store_sem,
    x_ss,
    x_rs,
    p_ss,
    p_rs,
    h_ss,
    h_rs,
    c_ss,
    c_rs,
    m_ss,
    m_rs,
    y_ss,
    y_rs,
    t_ss,
    t_rs,
    phase,
    told,
    go,
):
    n_blk, size = xv.shape[0], xv.shape[1]
    dp, bfly = lax.axis_index("dp"), lax.axis_index("bfly")
    core, y, xl = dp % 2, (dp // 2) % NY, dp // (2 * NY)
    z, xh = bfly // 2, bfly % 2
    z_dev = (dp, ((z + NZ // 2) % NZ) * 2 + xh)
    xh_dev = (dp, z * 2 + (1 - xh))
    core_dev = (dp + 1 - 2 * core, bfly)
    xl_dev = (((1 - xl) * NY + y) * 2 + core, bfly)

    ring = [(dp, ((z + j) % NZ) * 2 + xh) for j in range(1, NZ)]

    def y_dev(to):
        return ((xl * NY + to) * 2 + core, bfly)

    def remote(src, dst, ss, rs, dev):
        return pltpu.make_async_remote_copy(
            src_ref=src, dst_ref=dst, send_sem=ss, recv_sem=rs, device_id=dev, device_id_type=MESH
        )

    def cols(k):
        return pl.ds(k * size, size)

    half = NZ // 2
    low = z < half
    plane = [y_dev((y + j) % NY) for j in range(1, NY)] + [xh_dev, xl_dev, core_dev]
    known = plane + [(dp, ((z + j) % half) * 2 + xh) for j in range(1, half)]
    barrier = pltpu.get_barrier_semaphore()
    pl.semaphore_signal(barrier, inc=1, device_id=z_dev, device_id_type=MESH)

    @pl.when(low)
    def _():
        for dev in known:
            pl.semaphore_signal(barrier, inc=1, device_id=dev, device_id_type=MESH)

    load_g = [pltpu.make_async_copy(g_hbm.at[:, cols(k)], gv.at[k], load_sem.at[k]) for k in range(n_blk)]
    load_x = [
        pltpu.make_async_copy(x_hbm.at[:, cols(k)], xv.at[k], load_sem.at[n_blk + k]) for k in range(n_blk)
    ]
    load_wb = [pltpu.make_async_copy(wb_hbm.at[s], wbv.at[s], load_sem.at[2 * n_blk + s]) for s in range(2)]
    load_wa = [pltpu.make_async_copy(wa_hbm.at[s], wav.at[s], load_sem.at[2 * n_blk + 2 + s]) for s in range(2)]
    load_wb[1].start()
    for c in load_g:
        c.start()
    for c in load_x:
        c.start()
    load_wa[0].start()
    load_wb[0].start()
    load_wa[1].start()

    pl.semaphore_wait(barrier, jnp.where(low, 1 + len(known), 1))

    send_x = [remote(x_hbm.at[:, cols(k)], xp.at[k], x_ss.at[k], x_rs.at[k], z_dev) for k in range(n_blk)]
    send_p = [remote(ps.at[k], pr.at[k], p_ss.at[k], p_rs.at[k], xh_dev) for k in range(n_blk)]
    for c in send_x:
        c.start()
    @pl.when(low)
    def _():
        for dev in known:
            pl.semaphore_signal(told, inc=1, device_id=dev, device_id_type=MESH)

    load_wb[1].wait()
    for k in range(n_blk):
        load_g[k].wait()
        ps[k] = dot_nt(gv[k], wbv[1, k]).astype(BF16)

    @pl.when(jnp.logical_not(low))
    def _():
        pl.semaphore_wait(go, 1)

    for c in send_p:
        c.start()

    @pl.when(low)
    def _():
        pl.semaphore_wait(told, len(known))
        pl.semaphore_signal(go, inc=1, device_id=z_dev, device_id_type=MESH)

    send_h = [remote(hv.at[k], hp.at[k], h_ss.at[k], h_rs.at[k], xh_dev) for k in range(n_blk)]
    land_c = [cr.at[k] for k in range(n_blk - 1)] + [last_hbm]
    send_c = [remote(cs.at[k], land_c[k], c_ss.at[k], c_rs.at[k], z_dev) for k in range(n_blk)]
    send_m = [
        [
            remote(
                loc.at[k, pl.ds(2 * h, 2), :, :, 1 - core],
                sib.at[k, pl.ds(2 * h, 2)],
                m_ss.at[k, h],
                m_rs.at[k, h],
                core_dev,
            )
            for h in range(2)
        ]
        for k in range(n_blk)
    ]
    send_y = [
        [
            remote(
                ysend.at[k, (y + j) % NY],
                yrecv.at[k, j - 1],
                y_ss.at[k, j - 1],
                y_rs.at[k, j - 1],
                y_dev((y + j) % NY),
            )
            for j in range(1, NY)
        ]
        for k in range(n_blk)
    ]
    send_t = [remote(tsum.at[k, 1 - xl], trecv.at[k], t_ss.at[k], t_rs.at[k], xl_dev) for k in range(n_blk)]
    store_out = [
        pltpu.make_async_copy(outv.at[k], out_hbm.at[:, cols(k)], store_sem.at[k]) for k in range(n_blk)
    ]
    store_gi = [
        pltpu.make_async_copy(giv.at[k], gi_hbm.at[:, cols(k)], store_sem.at[n_blk + k])
        for k in range(n_blk - 1)
    ]
    store_ga = pltpu.make_async_copy(gav, ga_hbm, store_sem.at[2 * n_blk])
    store_own = pltpu.make_async_copy(own.at[n_blk - 1], own_hbm, store_sem.at[2 * n_blk - 1])
    store_gb = pltpu.make_async_copy(gbv, gb_hbm, store_sem.at[2 * n_blk + 1])

    def keep(k, m, value):
        loc[k, m] = value.reshape(loc.shape[2:])

    def first_factor(k):
        load_x[k].wait()
        if k == 0:
            load_wa[0].wait()
            load_wa[1].wait()
            load_wb[0].wait()
        dhf[...] = dot_nt(gv[k], wbv[0, k])
        uf[...] = dot_nn(xv[k], wav[0, k])
        send_x[k].wait_recv()
        if k == SIGNAL_AT:
            for dev in ring:
                pl.semaphore_signal(phase, inc=1, device_id=dev, device_id_type=MESH)
        uf[...] += dot_nn(xp[k], wav[1, k])
        send_p[k].wait_recv()

        def rows(i, _):
            at = pl.ds(pl.multiple_of(i * ROWS, ROWS), ROWS)
            u = uf[at, :]
            dh = dhf[at, :] + pr[k, at, :].astype(F32)
            phi = 0.5 + 0.5 * lax.erf(u * F32(0.5**0.5))
            dens = jnp.exp(u * u * F32(-0.5)) * F32(0.3989422804014327)
            hv[k, at, :] = (u * phi).astype(BF16)
            du[k, at, :] = (dh * (phi + u * dens)).astype(BF16)
            return 0

        lax.fori_loop(0, size // ROWS, rows, 0)
        send_h[k].start()
        cs[k] = dot_nt(du[k], wav[1, k]).astype(BF16)
        if k == n_blk - 1:
            send_c[k].start()
        keep(k, 0, dot_tn(xv[k], du[k]))
        keep(k, 1, dot_tn(xp[k], du[k]))
        send_m[k][0].start()
        own[k] = dot_nt(du[k], wav[0, k])
        if k == n_blk - 1:
            store_own.start()

    def second_factor(k):
        keep(k, 2, dot_tn(hv[k], gv[k]))
        mine = dot_nn(hv[k], wbv[0, k])
        send_h[k].wait_recv()
        keep(k, 3, dot_tn(hp[k], gv[k]))
        send_m[k][1].start()
        outv[k] = (mine + dot_nn(hp[k], wbv[1, k])).astype(BF16)
        store_out[k].start()

    def to_owners(k):
        for h in range(2):
            send_m[k][h].wait_recv()
        for m in range(4):
            both = [loc[k, m, s, :, core] + sib[k, m, s] for s in range(2)]
            ysend[k, :, m] = jnp.concatenate(both, axis=1).astype(BF16)
        for j in (4, 3, 5, 2, 6, 1, 7):
            send_y[k][j - 1].start()

    def sum_y(k):
        for j in range(1, NY):
            send_y[k][j - 1].wait_recv()
        for m in range(4):
            mine = [loc[k, m, s, y, core] + sib[k, m, s, y] for s in range(2)]
            total = jnp.concatenate(mine, axis=0)
            for j in range(NY - 1):
                total = total + yrecv[k, j, m].astype(F32)
            tsum[k, 0, m] = total[:8]
            tsum[k, 1, m] = total[8:]
        send_t[k].start()

    def finish_weights(k):
        send_t[k].wait_recv()
        for m in range(4):
            value = (tsum[k, xl, m] + trecv[k, m]) * scale
            into = gav if m < 2 else gbv
            for r in range(8):
                into[r, m % 2, pl.ds(k, 1), :] = value[r : r + 1, :]

    def finish_input(k):
        send_c[k].wait_recv()
        giv[k] = (own[k] + cr[k].astype(F32)).astype(BF16)
        store_gi[k].start()

    first_factor(0)
    first_factor(1)
    second_factor(0)
    first_factor(2)
    second_factor(1)
    to_owners(0)
    pl.semaphore_wait(phase, NZ - 1)
    for c in send_c[:3]:
        c.start()
    first_factor(3)
    second_factor(2)
    to_owners(1)
    sum_y(0)
    second_factor(3)
    to_owners(2)
    sum_y(1)
    finish_weights(0)
    to_owners(3)
    sum_y(2)
    finish_weights(1)
    finish_input(0)
    sum_y(3)
    finish_weights(2)
    finish_input(1)
    finish_weights(3)
    store_ga.start()
    store_gb.start()
    finish_input(2)
    for k in range(n_blk):
        for c in [send_x[k], send_p[k], send_h[k], *send_m[k], *send_y[k], send_t[k]]:
            c.wait_send()
        store_out[k].wait()
    store_ga.wait()
    store_gb.wait()
    for c in store_gi:
        c.wait()
    store_own.wait()
    for c in send_c:
        c.wait_send()
    send_c[3].wait_recv()


def shards(n_dp, tokens, weight_a, weight_b, upstream):
    rows, width = tokens.shape
    n_blk, size = weight_a.shape[1], weight_a.shape[2]
    own_rows = size // n_dp
    scale = float((rows * n_dp) ** -0.5)
    results = (
        jax.ShapeDtypeStruct((rows, width), BF16),
        jax.ShapeDtypeStruct((rows, width), BF16),
        jax.ShapeDtypeStruct((own_rows, 2, n_blk, size), F32),
        jax.ShapeDtypeStruct((own_rows, 2, n_blk, size), F32),
    )
    anywhere = pl.BlockSpec(memory_space=pl.ANY)
    act = pltpu.VMEM((n_blk, rows, size), BF16)
    weights = pltpu.VMEM((2, n_blk, size, size), BF16)
    dma = pltpu.SemaphoreType.DMA
    made = pl.pallas_call(
        functools.partial(main_kernel, scale),
        out_shape=(
            *results,
            jax.ShapeDtypeStruct((rows, size), F32),
            jax.ShapeDtypeStruct((rows, size), BF16),
        ),
        in_specs=[anywhere] * 4,
        out_specs=[anywhere] * 6,
        scratch_shapes=[
            act,
            act,
            weights,
            weights,
            act,
            act,
            act,
            act,
            act,
            act,
            act,
            pltpu.VMEM((rows, size), F32),
            pltpu.VMEM((rows, size), F32),
            act,
            pltpu.VMEM((n_blk, rows, size), F32),
            pltpu.VMEM((n_blk, 4, 2, NY, 2, own_rows, size), F32),
            pltpu.VMEM((n_blk, 4, 2, NY, own_rows, size), F32),
            pltpu.VMEM((n_blk, NY, 4, 2 * own_rows, size), BF16),
            pltpu.VMEM((n_blk, NY - 1, 4, 2 * own_rows, size), BF16),
            pltpu.VMEM((n_blk, 2, 4, own_rows, size), F32),
            pltpu.VMEM((n_blk, 4, own_rows, size), F32),
            act,
            act,
            pltpu.VMEM((own_rows, 2, n_blk, size), F32),
            pltpu.VMEM((own_rows, 2, n_blk, size), F32),
            dma((2 * n_blk + 4,)),
            dma((2 * n_blk + 2,)),
            dma((n_blk,)),
            dma((n_blk,)),
            dma((n_blk,)),
            dma((n_blk,)),
            dma((n_blk,)),
            dma((n_blk,)),
            dma((n_blk,)),
            dma((n_blk,)),
            dma((n_blk, 2)),
            dma((n_blk, 2)),
            dma((n_blk, NY - 1)),
            dma((n_blk, NY - 1)),
            dma((n_blk,)),
            dma((n_blk,)),
            pltpu.SemaphoreType.REGULAR,
            pltpu.SemaphoreType.REGULAR,
            pltpu.SemaphoreType.REGULAR,
        ],
        compiler_params=pltpu.CompilerParams(
            collective_id=0, has_side_effects=True, vmem_limit_bytes=60 << 20
        ),
    )(tokens, upstream, weight_a, weight_b)
    vm = pl.BlockSpec(memory_space=pltpu.VMEM)
    return pl.pallas_call(
        copy_kernel,
        out_shape=results,
        in_specs=[vm] * 6,
        out_specs=[vm] * 4,
    )(*made)


def copy_kernel(out, gi, ga, gb, own, last, out_to, gi_to, ga_to, gb_to):
    out_to[...] = out[...]
    ga_to[...] = ga[...]
    gb_to[...] = gb[...]
    done = gi.shape[1] - own.shape[1]
    gi_to[:, :done] = gi[:, :done]
    gi_to[:, done:] = (own[...] + last[...].astype(F32)).astype(BF16)


def solution(mesh):
    in_specs = (
        P("dp", "bfly"),
        P(None, "bfly", None, None),
        P(None, "bfly", None, None),
        P("dp", "bfly"),
    )
    out_specs = (
        P("dp", "bfly"),
        P("dp", "bfly"),
        P("dp", None, "bfly", None),
        P("dp", None, "bfly", None),
    )
    return jax.shard_map(
        functools.partial(shards, mesh.shape["dp"]),
        mesh=mesh,
        in_specs=in_specs,
        out_specs=out_specs,
        check_vma=False,
    )
```

```python
import functools

import jax
import jax.numpy as jnp
from jax import lax
from jax.experimental import pallas as pl
from jax.experimental.pallas import tpu as pltpu
from jax.sharding import PartitionSpec as P

MESH = pl.DeviceIdType.MESH
NY = 8
NZ = 8
F32 = jnp.float32
BF16 = jnp.bfloat16
SIGNAL_AT = 0
ROWS = 32


def dot_nn(a, b):
    return lax.dot_general(a, b, (((1,), (0,)), ((), ())), preferred_element_type=F32)


def dot_nt(a, b):
    return lax.dot_general(a, b, (((1,), (1,)), ((), ())), preferred_element_type=F32)


def dot_tn(a, b):
    return lax.dot_general(a, b, (((0,), (0,)), ((), ())), preferred_element_type=F32)


def main_kernel(
    scale,
    x_hbm,
    g_hbm,
    wa_hbm,
    wb_hbm,
    out_hbm,
    gi_hbm,
    ga_hbm,
    gb_hbm,
    own_hbm,
    last_hbm,
    xv,
    gv,
    wav,
    wbv,
    xp,
    ps,
    pr,
    hv,
    hp,
    cs,
    cr,
    uf,
    dhf,
    du,
    own,
    loc,
    sib,
    ysend,
    yrecv,
    tsend,
    trecv,
    outv,
    giv,
    gav,
    gbv,
    load_sem,
    store_sem,
    x_ss,
    x_rs,
    p_ss,
    p_rs,
    h_ss,
    h_rs,
    c_ss,
    c_rs,
    m_ss,
    m_rs,
    y_ss,
    y_rs,
    t_ss,
    t_rs,
    phase,
    told,
    go,
):
    n_blk, size = xv.shape[0], xv.shape[1]
    dp, bfly = lax.axis_index("dp"), lax.axis_index("bfly")
    core, y, xl = dp % 2, (dp // 2) % NY, dp // (2 * NY)
    z, xh = bfly // 2, bfly % 2
    z_dev = (dp, ((z + NZ // 2) % NZ) * 2 + xh)
    xh_dev = (dp, z * 2 + (1 - xh))
    core_dev = (dp + 1 - 2 * core, bfly)
    xl_dev = (((1 - xl) * NY + y) * 2 + core, bfly)

    ring = [(dp, ((z + j) % NZ) * 2 + xh) for j in (2, NZ - 2)]

    def y_dev(to):
        return ((xl * NY + to) * 2 + core, bfly)

    def remote(src, dst, ss, rs, dev):
        return pltpu.make_async_remote_copy(
            src_ref=src, dst_ref=dst, send_sem=ss, recv_sem=rs, device_id=dev, device_id_type=MESH
        )

    def cols(k):
        return pl.ds(k * size, size)

    half = NZ // 2
    low = z < half
    plane = [y_dev((y + j) % NY) for j in range(1, NY)] + [xh_dev, xl_dev, core_dev]
    known = plane + [(dp, ((z + j) % half) * 2 + xh) for j in range(1, half)]
    barrier = pltpu.get_barrier_semaphore()
    pl.semaphore_signal(barrier, inc=1, device_id=z_dev, device_id_type=MESH)

    @pl.when(low)
    def _():
        for dev in known:
            pl.semaphore_signal(barrier, inc=1, device_id=dev, device_id_type=MESH)

    load_g = [pltpu.make_async_copy(g_hbm.at[:, cols(k)], gv.at[k], load_sem.at[k]) for k in range(n_blk)]
    load_x = [
        pltpu.make_async_copy(x_hbm.at[:, cols(k)], xv.at[k], load_sem.at[n_blk + k]) for k in range(n_blk)
    ]
    load_wb = [pltpu.make_async_copy(wb_hbm.at[s], wbv.at[s], load_sem.at[2 * n_blk + s]) for s in range(2)]
    load_wa = [pltpu.make_async_copy(wa_hbm.at[s], wav.at[s], load_sem.at[2 * n_blk + 2 + s]) for s in range(2)]
    load_wb[1].start()
    for c in load_g:
        c.start()
    for c in load_x:
        c.start()
    load_wa[0].start()
    load_wb[0].start()
    load_wa[1].start()

    pl.semaphore_wait(barrier, jnp.where(low, 1 + len(known), 1))

    send_x = [remote(x_hbm.at[:, cols(k)], xp.at[k], x_ss.at[k], x_rs.at[k], z_dev) for k in range(n_blk)]
    send_p = [remote(ps.at[k], pr.at[k], p_ss.at[k], p_rs.at[k], xh_dev) for k in range(n_blk)]
    for c in send_x:
        c.start()
    @pl.when(low)
    def _():
        for dev in known:
            pl.semaphore_signal(told, inc=1, device_id=dev, device_id_type=MESH)

    load_wb[1].wait()
    for k in range(n_blk):
        load_g[k].wait()
        ps[k] = dot_nt(gv[k], wbv[1, k]).astype(BF16)

    @pl.when(jnp.logical_not(low))
    def _():
        pl.semaphore_wait(go, 1)

    for c in send_p:
        c.start()

    @pl.when(low)
    def _():
        pl.semaphore_wait(told, len(known))
        pl.semaphore_signal(go, inc=1, device_id=z_dev, device_id_type=MESH)

    send_h = [remote(hv.at[k], hp.at[k], h_ss.at[k], h_rs.at[k], xh_dev) for k in range(n_blk)]
    land_c = [cr.at[k] for k in range(n_blk - 1)] + [last_hbm]
    send_c = [remote(cs.at[k], land_c[k], c_ss.at[k], c_rs.at[k], z_dev) for k in range(n_blk)]
    send_m = [
        [
            remote(
                loc.at[k, pl.ds(2 * h, 2), :, :, 1 - core],
                sib.at[k, pl.ds(2 * h, 2)],
                m_ss.at[k, h],
                m_rs.at[k, h],
                core_dev,
            )
            for h in range(2)
        ]
        for k in range(n_blk)
    ]
    send_y = [
        [
            [
                remote(
                    ysend.at[k, h, (y + j) % NY],
                    yrecv.at[k, h, j - 1],
                    y_ss.at[k, h, j - 1],
                    y_rs.at[k, h, j - 1],
                    y_dev((y + j) % NY),
                )
                for j in range(1, NY)
            ]
            for h in range(2)
        ]
        for k in range(n_blk)
    ]
    send_t = [
        [remote(tsend.at[k, h], trecv.at[k, h], t_ss.at[k, h], t_rs.at[k, h], xl_dev) for h in range(2)]
        for k in range(n_blk)
    ]
    store_out = [
        pltpu.make_async_copy(outv.at[k], out_hbm.at[:, cols(k)], store_sem.at[k]) for k in range(n_blk)
    ]
    store_gi = [
        pltpu.make_async_copy(giv.at[k], gi_hbm.at[:, cols(k)], store_sem.at[n_blk + k])
        for k in range(n_blk - 1)
    ]
    store_ga = pltpu.make_async_copy(gav, ga_hbm, store_sem.at[2 * n_blk])
    store_own = pltpu.make_async_copy(own.at[n_blk - 1], own_hbm, store_sem.at[2 * n_blk - 1])
    store_gb = pltpu.make_async_copy(gbv, gb_hbm, store_sem.at[2 * n_blk + 1])

    def keep(k, m, value):
        loc[k, m] = value.reshape(loc.shape[2:])

    def first_factor(k):
        load_x[k].wait()
        if k == 0:
            load_wa[0].wait()
            load_wa[1].wait()
            load_wb[0].wait()
        dhf[...] = dot_nt(gv[k], wbv[0, k])
        uf[...] = dot_nn(xv[k], wav[0, k])
        send_x[k].wait_recv()
        if k == SIGNAL_AT:
            for dev in ring:
                pl.semaphore_signal(phase, inc=1, device_id=dev, device_id_type=MESH)
        uf[...] += dot_nn(xp[k], wav[1, k])
        send_p[k].wait_recv()

        def rows(i, _):
            at = pl.ds(pl.multiple_of(i * ROWS, ROWS), ROWS)
            u = uf[at, :]
            dh = dhf[at, :] + pr[k, at, :].astype(F32)
            phi = 0.5 + 0.5 * lax.erf(u * F32(0.5**0.5))
            dens = jnp.exp(u * u * F32(-0.5)) * F32(0.3989422804014327)
            hv[k, at, :] = (u * phi).astype(BF16)
            du[k, at, :] = (dh * (phi + u * dens)).astype(BF16)
            return 0

        lax.fori_loop(0, size // ROWS, rows, 0)
        send_h[k].start()
        cs[k] = dot_nt(du[k], wav[1, k]).astype(BF16)
        if k >= 2:
            send_c[k].start()
        keep(k, 0, dot_tn(xv[k], du[k]))
        keep(k, 1, dot_tn(xp[k], du[k]))
        send_m[k][0].start()
        own[k] = dot_nt(du[k], wav[0, k])
        if k == n_blk - 1:
            store_own.start()

    def second_factor(k):
        keep(k, 2, dot_tn(hv[k], gv[k]))
        mine = dot_nn(hv[k], wbv[0, k])
        send_h[k].wait_recv()
        keep(k, 3, dot_tn(hp[k], gv[k]))
        send_m[k][1].start()
        outv[k] = (mine + dot_nn(hp[k], wbv[1, k])).astype(BF16)
        store_out[k].start()

    def merged(k, h, s, at):
        return jnp.concatenate(
            [loc[k, m, s, at, core] + sib[k, m, s, at] for m in (2 * h, 2 * h + 1)], axis=-2
        )

    def to_half(k, h):
        send_m[k][h].wait_recv()
        tsend[k, h] = merged(k, h, 1 - xl, slice(None)).astype(BF16)
        send_t[k][h].start()

    def to_owners(k, h):
        send_t[k][h].wait_recv()
        ysend[k, h] = (merged(k, h, xl, slice(None)) + trecv[k, h].astype(F32)).astype(BF16)
        for j in (4, 3, 5, 2, 6, 1, 7):
            send_y[k][h][j - 1].start()

    def finish_weights(k, h):
        for j in range(1, NY):
            send_y[k][h][j - 1].wait_recv()
        total = merged(k, h, xl, y) + trecv[k, h, y].astype(F32)
        for j in range(NY - 1):
            total = total + yrecv[k, h, j].astype(F32)
        total = total * scale
        into = (gav, gbv)[h]
        for m in range(2):
            for r in range(8):
                at = 8 * m + r
                into[r, m, pl.ds(k, 1), :] = total[at : at + 1, :]

    def finish_input(k):
        send_c[k].wait_recv()
        giv[k] = (own[k] + cr[k].astype(F32)).astype(BF16)
        store_gi[k].start()

    first_factor(0)
    to_half(0, 0)
    first_factor(1)
    to_half(1, 0)
    pl.semaphore_wait(phase, len(ring))
    for c in send_c[:2]:
        c.start()
    first_factor(2)
    second_factor(0)
    to_half(2, 0)
    to_owners(0, 0)
    to_half(0, 1)
    second_factor(1)
    to_owners(1, 0)
    first_factor(3)
    to_half(1, 1)
    to_owners(0, 1)
    to_half(3, 0)
    second_factor(2)
    to_owners(2, 0)
    to_half(2, 1)
    to_owners(1, 1)
    finish_weights(0, 0)
    second_factor(3)
    to_owners(3, 0)
    to_half(3, 1)
    to_owners(2, 1)
    finish_weights(1, 0)
    finish_weights(0, 1)
    to_owners(3, 1)
    finish_weights(2, 0)
    finish_input(0)
    finish_weights(1, 1)
    finish_weights(3, 0)
    finish_input(1)
    finish_weights(2, 1)
    finish_input(2)
    finish_weights(3, 1)
    store_ga.start()
    store_gb.start()
    for k in range(n_blk):
        for c in [send_x[k], send_p[k], send_h[k], *send_m[k], *send_y[k][0], *send_y[k][1], *send_t[k]]:
            c.wait_send()
        store_out[k].wait()
    store_ga.wait()
    store_gb.wait()
    for c in store_gi:
        c.wait()
    store_own.wait()
    for c in send_c:
        c.wait_send()
    send_c[3].wait_recv()


def shards(n_dp, tokens, weight_a, weight_b, upstream):
    rows, width = tokens.shape
    n_blk, size = weight_a.shape[1], weight_a.shape[2]
    own_rows = size // n_dp
    scale = float((rows * n_dp) ** -0.5)
    results = (
        jax.ShapeDtypeStruct((rows, width), BF16),
        jax.ShapeDtypeStruct((rows, width), BF16),
        jax.ShapeDtypeStruct((own_rows, 2, n_blk, size), F32),
        jax.ShapeDtypeStruct((own_rows, 2, n_blk, size), F32),
    )
    anywhere = pl.BlockSpec(memory_space=pl.ANY)
    act = pltpu.VMEM((n_blk, rows, size), BF16)
    weights = pltpu.VMEM((2, n_blk, size, size), BF16)
    dma = pltpu.SemaphoreType.DMA
    made = pl.pallas_call(
        functools.partial(main_kernel, scale),
        out_shape=(
            *results,
            jax.ShapeDtypeStruct((rows, size), F32),
            jax.ShapeDtypeStruct((rows, size), BF16),
        ),
        in_specs=[anywhere] * 4,
        out_specs=[anywhere] * 6,
        scratch_shapes=[
            act,
            act,
            weights,
            weights,
            act,
            act,
            act,
            act,
            act,
            act,
            act,
            pltpu.VMEM((rows, size), F32),
            pltpu.VMEM((rows, size), F32),
            act,
            pltpu.VMEM((n_blk, rows, size), F32),
            pltpu.VMEM((n_blk, 4, 2, NY, 2, own_rows, size), F32),
            pltpu.VMEM((n_blk, 4, 2, NY, own_rows, size), F32),
            pltpu.VMEM((n_blk, 2, NY, 2 * own_rows, size), BF16),
            pltpu.VMEM((n_blk, 2, NY - 1, 2 * own_rows, size), BF16),
            pltpu.VMEM((n_blk, 2, NY, 2 * own_rows, size), BF16),
            pltpu.VMEM((n_blk, 2, NY, 2 * own_rows, size), BF16),
            act,
            act,
            pltpu.VMEM((own_rows, 2, n_blk, size), F32),
            pltpu.VMEM((own_rows, 2, n_blk, size), F32),
            dma((2 * n_blk + 4,)),
            dma((2 * n_blk + 2,)),
            dma((n_blk,)),
            dma((n_blk,)),
            dma((n_blk,)),
            dma((n_blk,)),
            dma((n_blk,)),
            dma((n_blk,)),
            dma((n_blk,)),
            dma((n_blk,)),
            dma((n_blk, 2)),
            dma((n_blk, 2)),
            dma((n_blk, 2, NY - 1)),
            dma((n_blk, 2, NY - 1)),
            dma((n_blk, 2)),
            dma((n_blk, 2)),
            pltpu.SemaphoreType.REGULAR,
            pltpu.SemaphoreType.REGULAR,
            pltpu.SemaphoreType.REGULAR,
        ],
        compiler_params=pltpu.CompilerParams(
            collective_id=0, has_side_effects=True, vmem_limit_bytes=60 << 20
        ),
    )(tokens, upstream, weight_a, weight_b)
    vm = pl.BlockSpec(memory_space=pltpu.VMEM)
    return pl.pallas_call(
        copy_kernel,
        out_shape=results,
        in_specs=[vm] * 6,
        out_specs=[vm] * 4,
    )(*made)


def copy_kernel(out, gi, ga, gb, own, last, out_to, gi_to, ga_to, gb_to):
    out_to[...] = out[...]
    ga_to[...] = ga[...]
    gb_to[...] = gb[...]
    done = gi.shape[1] - own.shape[1]
    gi_to[:, :done] = gi[:, :done]
    gi_to[:, done:] = (own[...] + last[...].astype(F32)).astype(BF16)


def solution(mesh):
    in_specs = (
        P("dp", "bfly"),
        P(None, "bfly", None, None),
        P(None, "bfly", None, None),
        P("dp", "bfly"),
    )
    out_specs = (
        P("dp", "bfly"),
        P("dp", "bfly"),
        P("dp", None, "bfly", None),
        P("dp", None, "bfly", None),
    )
    return jax.shard_map(
        functools.partial(shards, mesh.shape["dp"]),
        mesh=mesh,
        in_specs=in_specs,
        out_specs=out_specs,
        check_vma=False,
    )
```

```python
import functools

import jax
import jax.numpy as jnp
from jax import lax
from jax.experimental import pallas as pl
from jax.experimental.pallas import tpu as pltpu
from jax.sharding import PartitionSpec as P

MESH = pl.DeviceIdType.MESH
NY = 8
NZ = 8
F32 = jnp.float32
BF16 = jnp.bfloat16
ROWS = 32


def dot_nn(a, b):
    return lax.dot_general(a, b, (((1,), (0,)), ((), ())), preferred_element_type=F32)


def dot_nt(a, b):
    return lax.dot_general(a, b, (((1,), (1,)), ((), ())), preferred_element_type=F32)


def dot_tn(a, b):
    return lax.dot_general(a, b, (((0,), (0,)), ((), ())), preferred_element_type=F32)


def main_kernel(
    scale,
    x_hbm,
    g_hbm,
    wa_hbm,
    wb_hbm,
    outv,
    giv,
    gav,
    gbv,
    ownv,
    last,
    xv,
    gv,
    wav,
    wbv,
    xp,
    ps,
    pr,
    hv,
    hp,
    cs,
    cr,
    uf,
    dhf,
    du,
    own,
    loc,
    sib,
    asend,
    arecv,
    asum,
    frecv,
    ysend,
    yrecv,
    tsend,
    trecv,
    load_sem,
    x_ss,
    x_rs,
    p_ss,
    p_rs,
    h_ss,
    h_rs,
    c_ss,
    c_rs,
    m_ss,
    m_rs,
    a_ss,
    a_rs,
    f_ss,
    f_rs,
    y_ss,
    y_rs,
    t_ss,
    t_rs,
    told,
    go,
):
    n_blk, size = xv.shape[0], xv.shape[1]
    dp, bfly = lax.axis_index("dp"), lax.axis_index("bfly")
    core, y, xl = dp % 2, (dp // 2) % NY, dp // (2 * NY)
    z, xh = bfly // 2, bfly % 2
    z_dev = (dp, ((z + NZ // 2) % NZ) * 2 + xh)
    xh_dev = (dp, z * 2 + (1 - xh))
    core_dev = (dp + 1 - 2 * core, bfly)
    xl_dev = (((1 - xl) * NY + y) * 2 + core, bfly)


    def y_dev(to):
        return ((xl * NY + to) * 2 + core, bfly)

    def remote(src, dst, ss, rs, dev):
        return pltpu.make_async_remote_copy(
            src_ref=src, dst_ref=dst, send_sem=ss, recv_sem=rs, device_id=dev, device_id_type=MESH
        )

    def cols(k):
        return pl.ds(k * size, size)

    half = NZ // 2
    low = z < half
    plane = [y_dev((y + j) % NY) for j in range(1, NY)] + [xh_dev, xl_dev, core_dev]
    known = plane + [(dp, ((z + j) % half) * 2 + xh) for j in range(1, half)]
    barrier = pltpu.get_barrier_semaphore()
    pl.semaphore_signal(barrier, inc=1, device_id=z_dev, device_id_type=MESH)

    @pl.when(low)
    def _():
        for dev in known:
            pl.semaphore_signal(barrier, inc=1, device_id=dev, device_id_type=MESH)

    load_g = [pltpu.make_async_copy(g_hbm.at[:, cols(k)], gv.at[k], load_sem.at[k]) for k in range(n_blk)]
    load_x = [
        pltpu.make_async_copy(x_hbm.at[:, cols(k)], xv.at[k], load_sem.at[n_blk + k]) for k in range(n_blk)
    ]
    load_wb = [pltpu.make_async_copy(wb_hbm.at[s], wbv.at[s], load_sem.at[2 * n_blk + s]) for s in range(2)]
    load_wa = [pltpu.make_async_copy(wa_hbm.at[s], wav.at[s], load_sem.at[2 * n_blk + 2 + s]) for s in range(2)]
    load_wb[1].start()
    for c in load_g:
        c.start()
    for c in load_x:
        c.start()
    load_wa[0].start()
    load_wb[0].start()
    load_wa[1].start()

    pl.semaphore_wait(barrier, jnp.where(low, 1 + len(known), 1))

    send_x = [remote(x_hbm.at[:, cols(k)], xp.at[k], x_ss.at[k], x_rs.at[k], z_dev) for k in range(n_blk)]
    send_p = [remote(ps.at[k], pr.at[k], p_ss.at[k], p_rs.at[k], xh_dev) for k in range(n_blk)]
    for c in send_x:
        c.start()
    @pl.when(low)
    def _():
        for dev in known:
            pl.semaphore_signal(told, inc=1, device_id=dev, device_id_type=MESH)

    load_wb[1].wait()
    for k in range(n_blk):
        load_g[k].wait()
        ps[k] = dot_nt(gv[k], wbv[1, k]).astype(BF16)

    @pl.when(jnp.logical_not(low))
    def _():
        pl.semaphore_wait(go, 1)

    for c in send_p:
        c.start()

    @pl.when(low)
    def _():
        pl.semaphore_wait(told, len(known))
        pl.semaphore_signal(go, inc=1, device_id=z_dev, device_id_type=MESH)

    send_h = [remote(hv.at[k], hp.at[k], h_ss.at[k], h_rs.at[k], xh_dev) for k in range(n_blk)]
    land_c = [cr.at[k] for k in range(n_blk - 1)] + [last]
    send_c = [remote(cs.at[k], land_c[k], c_ss.at[k], c_rs.at[k], z_dev) for k in range(n_blk)]
    send_m = [
        [
            remote(
                loc.at[k, pl.ds(2 * h, 2), :, :, 1 - core],
                sib.at[k, pl.ds(2 * h, 2)],
                m_ss.at[k, h],
                m_rs.at[k, h],
                core_dev,
            )
            for h in range(2)
        ]
        for k in range(n_blk)
    ]
    send_a, send_y = (
        [
            [
                remote(
                    src.at[k, (y + j) % NY],
                    dst.at[k, j - 1],
                    ss.at[k, j - 1],
                    rs.at[k, j - 1],
                    y_dev((y + j) % NY),
                )
                for j in range(1, NY)
            ]
            for k in range(n_blk)
        ]
        for src, dst, ss, rs in ((asend, arecv, a_ss, a_rs), (ysend, yrecv, y_ss, y_rs))
    )
    send_t = [remote(tsend.at[k], trecv.at[k], t_ss.at[k], t_rs.at[k], xl_dev) for k in range(n_blk)]
    send_f = [
        remote(asum.at[k, 1 - xl], frecv.at[k], f_ss.at[k], f_rs.at[k], xl_dev) for k in range(n_blk)
    ]

    def keep(k, m, value):
        loc[k, m] = value.reshape(loc.shape[2:])

    def first_factor(k):
        load_x[k].wait()
        if k == 0:
            load_wa[0].wait()
            load_wa[1].wait()
            load_wb[0].wait()
        dhf[...] = dot_nt(gv[k], wbv[0, k])
        uf[...] = dot_nn(xv[k], wav[0, k])
        send_x[k].wait_recv()
        uf[...] += dot_nn(xp[k], wav[1, k])
        send_p[k].wait_recv()

        def rows(i, _):
            at = pl.ds(pl.multiple_of(i * ROWS, ROWS), ROWS)
            u = uf[at, :]
            dh = dhf[at, :] + pr[k, at, :].astype(F32)
            phi = 0.5 + 0.5 * lax.erf(u * F32(0.5**0.5))
            dens = jnp.exp(u * u * F32(-0.5)) * F32(0.3989422804014327)
            hv[k, at, :] = (u * phi).astype(BF16)
            du[k, at, :] = (dh * (phi + u * dens)).astype(BF16)
            return 0

        lax.fori_loop(0, size // ROWS, rows, 0)
        send_h[k].start()
        cs[k] = dot_nt(du[k], wav[1, k]).astype(BF16)
        if k >= 2:
            send_c[k].start()
        keep(k, 0, dot_tn(xv[k], du[k]))
        keep(k, 1, dot_tn(xp[k], du[k]))
        send_m[k][0].start()
        if k < n_blk - 1:
            own[k] = dot_nt(du[k], wav[0, k])
        else:
            ownv[...] = dot_nt(du[k], wav[0, k])

    def second_factor(k):
        keep(k, 2, dot_tn(hv[k], gv[k]))
        mine = dot_nn(hv[k], wbv[0, k])
        send_h[k].wait_recv()
        keep(k, 3, dot_tn(hp[k], gv[k]))
        send_m[k][1].start()
        outv[:, cols(k)] = (mine + dot_nn(hp[k], wbv[1, k])).astype(BF16)

    def merged(k, h, s, at):
        return jnp.concatenate(
            [loc[k, m, s, at, core] + sib[k, m, s, at] for m in (2 * h, 2 * h + 1)], axis=-2
        )

    def a_to_owners(k):
        send_m[k][0].wait_recv()
        halves = [merged(k, 0, s, slice(None)) for s in range(2)]
        asend[k] = jnp.concatenate(halves, axis=1).astype(BF16)
        for j in (4, 3, 5, 2, 6, 1, 7):
            send_a[k][j - 1].start()

    def a_sum(k):
        for j in range(1, NY):
            send_a[k][j - 1].wait_recv()
        total = jnp.concatenate([merged(k, 0, s, y) for s in range(2)], axis=0)
        for j in range(NY - 1):
            total = total + arecv[k, j].astype(F32)
        asum[k] = total.reshape(asum.shape[1:])
        send_f[k].start()

    def a_finish(k):
        send_f[k].wait_recv()
        put(k, gav, asum[k, xl] + frecv[k])

    def b_to_half(k):
        send_m[k][1].wait_recv()
        tsend[k] = merged(k, 1, 1 - xl, slice(None)).astype(BF16)
        send_t[k].start()

    def b_to_owners(k):
        send_t[k].wait_recv()
        ysend[k] = (merged(k, 1, xl, slice(None)) + trecv[k].astype(F32)).astype(BF16)
        for j in (4, 3, 5, 2, 6, 1, 7):
            send_y[k][j - 1].start()

    def b_finish(k):
        for j in range(1, NY):
            send_y[k][j - 1].wait_recv()
        total = merged(k, 1, xl, y) + trecv[k, y].astype(F32)
        for j in range(NY - 1):
            total = total + yrecv[k, j].astype(F32)
        put(k, gbv, total)

    def put(k, into, total):
        total = total * scale
        for m in range(2):
            for r in range(8):
                at = 8 * m + r
                into[r, m, pl.ds(k, 1), :] = total[at : at + 1, :]

    def finish_input(k):
        send_c[k].wait_recv()
        giv[:, cols(k)] = (own[k] + cr[k].astype(F32)).astype(BF16)

    first_factor(0)
    a_to_owners(0)
    first_factor(1)
    a_to_owners(1)
    for c in send_c[:2]:
        c.start()
    first_factor(2)
    second_factor(0)
    a_to_owners(2)
    b_to_half(0)
    second_factor(1)
    first_factor(3)
    b_to_half(1)
    b_to_owners(0)
    a_to_owners(3)
    second_factor(2)
    b_to_half(2)
    b_to_owners(1)
    a_sum(0)
    second_factor(3)
    a_sum(1)
    a_finish(0)
    b_to_half(3)
    b_to_owners(2)
    a_sum(2)
    b_finish(0)
    a_finish(1)
    b_to_owners(3)
    a_sum(3)
    finish_input(0)
    b_finish(1)
    a_finish(2)
    finish_input(1)
    b_finish(2)
    a_finish(3)
    finish_input(2)
    b_finish(3)
    for k in range(n_blk):
        for c in [send_x[k], send_p[k], send_h[k], *send_m[k], *send_a[k], *send_y[k], send_t[k], send_f[k]]:
            c.wait_send()
    for c in send_c:
        c.wait_send()
    send_c[3].wait_recv()


def shards(n_dp, tokens, weight_a, weight_b, upstream):
    rows, width = tokens.shape
    n_blk, size = weight_a.shape[1], weight_a.shape[2]
    own_rows = size // n_dp
    scale = float((rows * n_dp) ** -0.5)
    results = (
        jax.ShapeDtypeStruct((rows, width), BF16),
        jax.ShapeDtypeStruct((rows, width), BF16),
        jax.ShapeDtypeStruct((own_rows, 2, n_blk, size), F32),
        jax.ShapeDtypeStruct((own_rows, 2, n_blk, size), F32),
    )
    anywhere = pl.BlockSpec(memory_space=pl.ANY)
    act = pltpu.VMEM((n_blk, rows, size), BF16)
    weights = pltpu.VMEM((2, n_blk, size, size), BF16)
    dma = pltpu.SemaphoreType.DMA
    made = pl.pallas_call(
        functools.partial(main_kernel, scale),
        out_shape=(
            pltpu.VMEM((rows, width), BF16),
            pltpu.VMEM((rows, width - size), BF16),
            pltpu.VMEM((own_rows, 2, n_blk, size), F32),
            pltpu.VMEM((own_rows, 2, n_blk, size), F32),
            pltpu.VMEM((rows, size), F32),
            pltpu.VMEM((rows, size), BF16),
        ),
        in_specs=[anywhere] * 4,
        out_specs=[pl.BlockSpec(memory_space=pltpu.VMEM)] * 6,
        scratch_shapes=[
            act,
            act,
            weights,
            weights,
            act,
            act,
            act,
            act,
            act,
            act,
            act,
            pltpu.VMEM((rows, size), F32),
            pltpu.VMEM((rows, size), F32),
            act,
            pltpu.VMEM((n_blk, rows, size), F32),
            pltpu.VMEM((n_blk, 4, 2, NY, 2, own_rows, size), F32),
            pltpu.VMEM((n_blk, 4, 2, NY, own_rows, size), F32),
            pltpu.VMEM((n_blk, NY, 4 * own_rows, size), BF16),
            pltpu.VMEM((n_blk, NY - 1, 4 * own_rows, size), BF16),
            pltpu.VMEM((n_blk, 2, 2 * own_rows, size), F32),
            pltpu.VMEM((n_blk, 2 * own_rows, size), F32),
            pltpu.VMEM((n_blk, NY, 2 * own_rows, size), BF16),
            pltpu.VMEM((n_blk, NY - 1, 2 * own_rows, size), BF16),
            pltpu.VMEM((n_blk, NY, 2 * own_rows, size), BF16),
            pltpu.VMEM((n_blk, NY, 2 * own_rows, size), BF16),
            dma((2 * n_blk + 4,)),
            dma((n_blk,)),
            dma((n_blk,)),
            dma((n_blk,)),
            dma((n_blk,)),
            dma((n_blk,)),
            dma((n_blk,)),
            dma((n_blk,)),
            dma((n_blk,)),
            dma((n_blk, 2)),
            dma((n_blk, 2)),
            dma((n_blk, NY - 1)),
            dma((n_blk, NY - 1)),
            dma((n_blk,)),
            dma((n_blk,)),
            dma((n_blk, NY - 1)),
            dma((n_blk, NY - 1)),
            dma((n_blk,)),
            dma((n_blk,)),
            pltpu.SemaphoreType.REGULAR,
            pltpu.SemaphoreType.REGULAR,
        ],
        compiler_params=pltpu.CompilerParams(
            collective_id=0, has_side_effects=True, vmem_limit_bytes=40 << 20
        ),
    )(*[pltpu.with_memory_space_constraint(a, pltpu.HBM) for a in (tokens, upstream, weight_a, weight_b)])
    return pl.pallas_call(
        copy_kernel,
        out_shape=results,
        in_specs=[anywhere] * 4 + [pl.BlockSpec(memory_space=pltpu.VMEM)] * 2,
        out_specs=[anywhere] * 4,
        scratch_shapes=[pltpu.VMEM((rows, size), BF16), dma((5,))],
    )(*[pltpu.with_memory_space_constraint(a, pltpu.VMEM) for a in made])


def copy_kernel(out, gi, ga, gb, own, last, out_to, gi_to, ga_to, gb_to, block, sems):
    done = gi.shape[1]
    copies = [
        pltpu.make_async_copy(out, out_to, sems.at[0]),
        pltpu.make_async_copy(gi, gi_to.at[:, pl.ds(0, done)], sems.at[1]),
        pltpu.make_async_copy(ga, ga_to, sems.at[2]),
        pltpu.make_async_copy(gb, gb_to, sems.at[3]),
        pltpu.make_async_copy(block, gi_to.at[:, pl.ds(done, block.shape[1])], sems.at[4]),
    ]
    for c in copies[:4]:
        c.start()
    block[...] = (own[...] + last[...].astype(F32)).astype(BF16)
    copies[4].start()
    for c in copies:
        c.wait()


def solution(mesh):
    in_specs = (
        P("dp", "bfly"),
        P(None, "bfly", None, None),
        P(None, "bfly", None, None),
        P("dp", "bfly"),
    )
    out_specs = (
        P("dp", "bfly"),
        P("dp", "bfly"),
        P("dp", None, "bfly", None),
        P("dp", None, "bfly", None),
    )
    return jax.shard_map(
        functools.partial(shards, mesh.shape["dp"]),
        mesh=mesh,
        in_specs=in_specs,
        out_specs=out_specs,
        check_vma=False,
    )
```

```python
import functools

import jax
import jax.numpy as jnp
from jax import lax
from jax.experimental import pallas as pl
from jax.experimental.pallas import tpu as pltpu
from jax.sharding import PartitionSpec as P

MESH = pl.DeviceIdType.MESH
NY = 8
NZ = 8
F32 = jnp.float32
BF16 = jnp.bfloat16
ROWS = 32


def dot_nn(a, b):
    return lax.dot_general(a, b, (((1,), (0,)), ((), ())), preferred_element_type=F32)


def dot_nt(a, b):
    return lax.dot_general(a, b, (((1,), (1,)), ((), ())), preferred_element_type=F32)


def dot_tn(a, b):
    return lax.dot_general(a, b, (((0,), (0,)), ((), ())), preferred_element_type=F32)


def main_kernel(
    scale,
    x_hbm,
    g_hbm,
    wa_hbm,
    wb_hbm,
    outv,
    giv,
    gav,
    gbv,
    ownv,
    last,
    xv,
    gv,
    wav,
    wbv,
    xp,
    ps,
    pr,
    hv,
    hp,
    cs,
    cr,
    uf,
    dhf,
    du,
    own,
    loc,
    sib,
    asend,
    arecv,
    asum,
    frecv,
    ysend,
    yrecv,
    tsend,
    trecv,
    load_sem,
    x_ss,
    x_rs,
    p_ss,
    p_rs,
    h_ss,
    h_rs,
    c_ss,
    c_rs,
    m_ss,
    m_rs,
    a_ss,
    a_rs,
    f_ss,
    f_rs,
    y_ss,
    y_rs,
    t_ss,
    t_rs,
    told,
    go,
):
    n_blk, size = xv.shape[0], xv.shape[1]
    dp, bfly = lax.axis_index("dp"), lax.axis_index("bfly")
    core, y, xl = dp % 2, (dp // 2) % NY, dp // (2 * NY)
    z, xh = bfly // 2, bfly % 2
    z_dev = (dp, ((z + NZ // 2) % NZ) * 2 + xh)
    xh_dev = (dp, z * 2 + (1 - xh))
    core_dev = (dp + 1 - 2 * core, bfly)
    xl_dev = (((1 - xl) * NY + y) * 2 + core, bfly)


    def y_dev(to):
        return ((xl * NY + to) * 2 + core, bfly)

    def remote(src, dst, ss, rs, dev):
        return pltpu.make_async_remote_copy(
            src_ref=src, dst_ref=dst, send_sem=ss, recv_sem=rs, device_id=dev, device_id_type=MESH
        )

    def cols(k):
        return pl.ds(k * size, size)

    half = NZ // 2
    low = z < half
    plane = [y_dev((y + j) % NY) for j in range(1, NY)] + [xh_dev, xl_dev, core_dev]
    known = plane + [(dp, ((z + j) % half) * 2 + xh) for j in range(1, half)]
    barrier = pltpu.get_barrier_semaphore()
    pl.semaphore_signal(barrier, inc=1, device_id=z_dev, device_id_type=MESH)

    @pl.when(low)
    def _():
        for dev in known:
            pl.semaphore_signal(barrier, inc=1, device_id=dev, device_id_type=MESH)

    load_g = [pltpu.make_async_copy(g_hbm.at[:, cols(k)], gv.at[k], load_sem.at[k]) for k in range(n_blk)]
    load_x = [
        pltpu.make_async_copy(x_hbm.at[:, cols(k)], xv.at[k], load_sem.at[n_blk + k]) for k in range(n_blk)
    ]
    load_wb = [pltpu.make_async_copy(wb_hbm.at[s], wbv.at[s], load_sem.at[2 * n_blk + s]) for s in range(2)]
    load_wa = [pltpu.make_async_copy(wa_hbm.at[s], wav.at[s], load_sem.at[2 * n_blk + 2 + s]) for s in range(2)]
    pl.semaphore_wait(barrier, jnp.where(low, 1 + len(known), 1))

    send_x = [remote(x_hbm.at[:, cols(k)], xp.at[k], x_ss.at[k], x_rs.at[k], z_dev) for k in range(n_blk)]
    send_p = [remote(ps.at[k], pr.at[k], p_ss.at[k], p_rs.at[k], xh_dev) for k in range(n_blk)]
    for c in send_x:
        c.start()
    load_wb[1].start()
    for c in load_g:
        c.start()
    for c in load_x:
        c.start()
    load_wa[0].start()
    load_wb[0].start()
    load_wa[1].start()
    @pl.when(low)
    def _():
        for dev in known:
            pl.semaphore_signal(told, inc=1, device_id=dev, device_id_type=MESH)

    load_wb[1].wait()
    for k in range(n_blk):
        load_g[k].wait()
        ps[k] = dot_nt(gv[k], wbv[1, k]).astype(BF16)

    @pl.when(jnp.logical_not(low))
    def _():
        pl.semaphore_wait(go, 1)

    for c in send_p:
        c.start()

    @pl.when(low)
    def _():
        pl.semaphore_wait(told, len(known))
        pl.semaphore_signal(go, inc=1, device_id=z_dev, device_id_type=MESH)

    send_h = [remote(hv.at[k], hp.at[k], h_ss.at[k], h_rs.at[k], xh_dev) for k in range(n_blk)]
    land_c = [cr.at[k] for k in range(n_blk - 1)] + [last]
    send_c = [remote(cs.at[k], land_c[k], c_ss.at[k], c_rs.at[k], z_dev) for k in range(n_blk)]
    send_m = [
        [
            remote(
                loc.at[k, pl.ds(2 * h, 2), :, :, 1 - core],
                sib.at[k, pl.ds(2 * h, 2)],
                m_ss.at[k, h],
                m_rs.at[k, h],
                core_dev,
            )
            for h in range(2)
        ]
        for k in range(n_blk)
    ]
    send_a, send_y = (
        [
            [
                remote(
                    src.at[k, (y + j) % NY],
                    dst.at[k, j - 1],
                    ss.at[k, j - 1],
                    rs.at[k, j - 1],
                    y_dev((y + j) % NY),
                )
                for j in range(1, NY)
            ]
            for k in range(n_blk)
        ]
        for src, dst, ss, rs in ((asend, arecv, a_ss, a_rs), (ysend, yrecv, y_ss, y_rs))
    )
    send_t = [remote(tsend.at[k], trecv.at[k], t_ss.at[k], t_rs.at[k], xl_dev) for k in range(n_blk)]
    send_f = [
        remote(asum.at[k, 1 - xl], frecv.at[k], f_ss.at[k], f_rs.at[k], xl_dev) for k in range(n_blk)
    ]

    hold = jnp.where(z == 7, 2, jnp.where(z == 4, 2, jnp.where(z == 2, 3, jnp.where(z == 0, 2, 1))))

    def keep(k, m, value):
        loc[k, m] = value.reshape(loc.shape[2:])

    def first_factor(k):
        load_x[k].wait()
        if k == 0:
            load_wa[0].wait()
            load_wa[1].wait()
            load_wb[0].wait()
        dhf[...] = dot_nt(gv[k], wbv[0, k])
        uf[...] = dot_nn(xv[k], wav[0, k])
        send_x[k].wait_recv()
        uf[...] += dot_nn(xp[k], wav[1, k])
        send_p[k].wait_recv()

        def rows(i, _):
            at = pl.ds(pl.multiple_of(i * ROWS, ROWS), ROWS)
            u = uf[at, :]
            dh = dhf[at, :] + pr[k, at, :].astype(F32)
            phi = 0.5 + 0.5 * lax.erf(u * F32(0.5**0.5))
            dens = jnp.exp(u * u * F32(-0.5)) * F32(0.3989422804014327)
            hv[k, at, :] = (u * phi).astype(BF16)
            du[k, at, :] = (dh * (phi + u * dens)).astype(BF16)
            return 0

        lax.fori_loop(0, size // ROWS, rows, 0)
        send_h[k].start()
        cs[k] = dot_nt(du[k], wav[1, k]).astype(BF16)

        @pl.when(hold == k)
        def _():
            for c in send_c[: k + 1]:
                c.start()

        @pl.when(hold < k)
        def _():
            send_c[k].start()

        keep(k, 0, dot_tn(xv[k], du[k]))
        keep(k, 1, dot_tn(xp[k], du[k]))
        send_m[k][0].start()
        if k < n_blk - 1:
            own[k] = dot_nt(du[k], wav[0, k])
        else:
            ownv[...] = dot_nt(du[k], wav[0, k])

    def second_factor(k):
        keep(k, 2, dot_tn(hv[k], gv[k]))
        mine = dot_nn(hv[k], wbv[0, k])
        send_h[k].wait_recv()
        keep(k, 3, dot_tn(hp[k], gv[k]))
        send_m[k][1].start()
        outv[:, cols(k)] = (mine + dot_nn(hp[k], wbv[1, k])).astype(BF16)

    def merged(k, h, s, at):
        return jnp.concatenate(
            [loc[k, m, s, at, core] + sib[k, m, s, at] for m in (2 * h, 2 * h + 1)], axis=-2
        )

    def a_to_owners(k):
        send_m[k][0].wait_recv()
        halves = [merged(k, 0, s, slice(None)) for s in range(2)]
        asend[k] = jnp.concatenate(halves, axis=1).astype(BF16)
        for j in (4, 3, 5, 2, 6, 1, 7):
            send_a[k][j - 1].start()

    def a_sum(k):
        for j in range(1, NY):
            send_a[k][j - 1].wait_recv()
        total = jnp.concatenate([merged(k, 0, s, y) for s in range(2)], axis=0)
        for j in range(NY - 1):
            total = total + arecv[k, j].astype(F32)
        asum[k] = total.reshape(asum.shape[1:])
        send_f[k].start()

    def a_finish(k):
        send_f[k].wait_recv()
        put(k, gav, asum[k, xl] + frecv[k])

    def b_to_half(k):
        send_m[k][1].wait_recv()
        tsend[k] = merged(k, 1, 1 - xl, slice(None)).astype(BF16)
        send_t[k].start()

    def b_to_owners(k):
        send_t[k].wait_recv()
        ysend[k] = (merged(k, 1, xl, slice(None)) + trecv[k].astype(F32)).astype(BF16)
        for j in (4, 3, 5, 2, 6, 1, 7):
            send_y[k][j - 1].start()

    def b_finish(k):
        for j in range(1, NY):
            send_y[k][j - 1].wait_recv()
        total = merged(k, 1, xl, y) + trecv[k, y].astype(F32)
        for j in range(NY - 1):
            total = total + yrecv[k, j].astype(F32)
        put(k, gbv, total)

    def put(k, into, total):
        total = total * scale
        for m in range(2):
            for r in range(8):
                at = 8 * m + r
                into[r, m, pl.ds(k, 1), :] = total[at : at + 1, :]

    def finish_input(k):
        send_c[k].wait_recv()
        giv[:, cols(k)] = (own[k] + cr[k].astype(F32)).astype(BF16)

    first_factor(0)
    a_to_owners(0)
    first_factor(1)
    a_to_owners(1)
    first_factor(2)
    second_factor(0)
    a_to_owners(2)
    b_to_half(0)
    second_factor(1)
    first_factor(3)
    b_to_half(1)
    b_to_owners(0)
    a_to_owners(3)
    second_factor(2)
    b_to_half(2)
    b_to_owners(1)
    a_sum(0)
    second_factor(3)
    a_sum(1)
    a_finish(0)
    b_to_half(3)
    b_to_owners(2)
    a_sum(2)
    b_finish(0)
    a_finish(1)
    b_to_owners(3)
    a_sum(3)
    finish_input(0)
    b_finish(1)
    a_finish(2)
    finish_input(1)
    b_finish(2)
    a_finish(3)
    finish_input(2)
    b_finish(3)
    for k in range(n_blk):
        for c in [send_x[k], send_p[k], send_h[k], *send_m[k], *send_a[k], *send_y[k], send_t[k], send_f[k]]:
            c.wait_send()
    for c in send_c:
        c.wait_send()
    send_c[3].wait_recv()


def shards(n_dp, tokens, weight_a, weight_b, upstream):
    rows, width = tokens.shape
    n_blk, size = weight_a.shape[1], weight_a.shape[2]
    own_rows = size // n_dp
    scale = float((rows * n_dp) ** -0.5)
    results = (
        jax.ShapeDtypeStruct((rows, width), BF16),
        jax.ShapeDtypeStruct((rows, width), BF16),
        jax.ShapeDtypeStruct((own_rows, 2, n_blk, size), F32),
        jax.ShapeDtypeStruct((own_rows, 2, n_blk, size), F32),
    )
    anywhere = pl.BlockSpec(memory_space=pl.ANY)
    act = pltpu.VMEM((n_blk, rows, size), BF16)
    weights = pltpu.VMEM((2, n_blk, size, size), BF16)
    dma = pltpu.SemaphoreType.DMA
    made = pl.pallas_call(
        functools.partial(main_kernel, scale),
        out_shape=(
            pltpu.VMEM((rows, width), BF16),
            pltpu.VMEM((rows, width - size), BF16),
            pltpu.VMEM((own_rows, 2, n_blk, size), F32),
            pltpu.VMEM((own_rows, 2, n_blk, size), F32),
            pltpu.VMEM((rows, size), F32),
            pltpu.VMEM((rows, size), BF16),
        ),
        in_specs=[anywhere] * 4,
        out_specs=[pl.BlockSpec(memory_space=pltpu.VMEM)] * 6,
        scratch_shapes=[
            act,
            act,
            weights,
            weights,
            act,
            act,
            act,
            act,
            act,
            act,
            act,
            pltpu.VMEM((rows, size), F32),
            pltpu.VMEM((rows, size), F32),
            act,
            pltpu.VMEM((n_blk, rows, size), F32),
            pltpu.VMEM((n_blk, 4, 2, NY, 2, own_rows, size), F32),
            pltpu.VMEM((n_blk, 4, 2, NY, own_rows, size), F32),
            pltpu.VMEM((n_blk, NY, 4 * own_rows, size), BF16),
            pltpu.VMEM((n_blk, NY - 1, 4 * own_rows, size), BF16),
            pltpu.VMEM((n_blk, 2, 2 * own_rows, size), F32),
            pltpu.VMEM((n_blk, 2 * own_rows, size), F32),
            pltpu.VMEM((n_blk, NY, 2 * own_rows, size), BF16),
            pltpu.VMEM((n_blk, NY - 1, 2 * own_rows, size), BF16),
            pltpu.VMEM((n_blk, NY, 2 * own_rows, size), BF16),
            pltpu.VMEM((n_blk, NY, 2 * own_rows, size), BF16),
            dma((2 * n_blk + 4,)),
            dma((n_blk,)),
            dma((n_blk,)),
            dma((n_blk,)),
            dma((n_blk,)),
            dma((n_blk,)),
            dma((n_blk,)),
            dma((n_blk,)),
            dma((n_blk,)),
            dma((n_blk, 2)),
            dma((n_blk, 2)),
            dma((n_blk, NY - 1)),
            dma((n_blk, NY - 1)),
            dma((n_blk,)),
            dma((n_blk,)),
            dma((n_blk, NY - 1)),
            dma((n_blk, NY - 1)),
            dma((n_blk,)),
            dma((n_blk,)),
            pltpu.SemaphoreType.REGULAR,
            pltpu.SemaphoreType.REGULAR,
        ],
        compiler_params=pltpu.CompilerParams(
            collective_id=0, has_side_effects=True, vmem_limit_bytes=40 << 20
        ),
    )(*[pltpu.with_memory_space_constraint(a, pltpu.HBM) for a in (tokens, upstream, weight_a, weight_b)])
    return pl.pallas_call(
        copy_kernel,
        out_shape=results,
        in_specs=[anywhere] * 4 + [pl.BlockSpec(memory_space=pltpu.VMEM)] * 2,
        out_specs=[anywhere] * 4,
        scratch_shapes=[pltpu.VMEM((rows, size), BF16), dma((5,))],
    )(*[pltpu.with_memory_space_constraint(a, pltpu.VMEM) for a in made])


def copy_kernel(out, gi, ga, gb, own, last, out_to, gi_to, ga_to, gb_to, block, sems):
    done = gi.shape[1]
    copies = [
        pltpu.make_async_copy(out, out_to, sems.at[0]),
        pltpu.make_async_copy(gi, gi_to.at[:, pl.ds(0, done)], sems.at[1]),
        pltpu.make_async_copy(ga, ga_to, sems.at[2]),
        pltpu.make_async_copy(gb, gb_to, sems.at[3]),
        pltpu.make_async_copy(block, gi_to.at[:, pl.ds(done, block.shape[1])], sems.at[4]),
    ]
    for c in copies[:4]:
        c.start()
    block[...] = (own[...] + last[...].astype(F32)).astype(BF16)
    copies[4].start()
    for c in copies:
        c.wait()


def solution(mesh):
    in_specs = (
        P("dp", "bfly"),
        P(None, "bfly", None, None),
        P(None, "bfly", None, None),
        P("dp", "bfly"),
    )
    out_specs = (
        P("dp", "bfly"),
        P("dp", "bfly"),
        P("dp", None, "bfly", None),
        P("dp", None, "bfly", None),
    )
    return jax.shard_map(
        functools.partial(shards, mesh.shape["dp"]),
        mesh=mesh,
        in_specs=in_specs,
        out_specs=out_specs,
        check_vma=False,
    )
```

```python
import functools

import jax
import jax.numpy as jnp
from jax import lax
from jax.experimental import pallas as pl
from jax.experimental.pallas import tpu as pltpu
from jax.sharding import PartitionSpec as P

MESH = pl.DeviceIdType.MESH
NY = 8
NZ = 8
F32 = jnp.float32
BF16 = jnp.bfloat16
ROWS = 32


def dot_nn(a, b):
    return lax.dot_general(a, b, (((1,), (0,)), ((), ())), preferred_element_type=F32)


def dot_nt(a, b):
    return lax.dot_general(a, b, (((1,), (1,)), ((), ())), preferred_element_type=F32)


def dot_tn(a, b):
    return lax.dot_general(a, b, (((0,), (0,)), ((), ())), preferred_element_type=F32)


def main_kernel(
    scale,
    x_hbm,
    g_hbm,
    wa_hbm,
    wb_hbm,
    outv,
    giv,
    gav,
    gbv,
    ownv,
    last,
    xv,
    gv,
    wav,
    wbv,
    xp,
    ps,
    pr,
    hv,
    hp,
    cs,
    cr,
    uf,
    dhf,
    du,
    own,
    loc,
    sib,
    asend,
    arecv,
    asum,
    frecv,
    ysend,
    yrecv,
    tsend,
    trecv,
    load_sem,
    x_ss,
    x_rs,
    p_ss,
    p_rs,
    h_ss,
    h_rs,
    c_ss,
    c_rs,
    m_ss,
    m_rs,
    a_ss,
    a_rs,
    f_ss,
    f_rs,
    y_ss,
    y_rs,
    t_ss,
    t_rs,
    told,
    go,
):
    n_blk, size = xv.shape[0], xv.shape[1]
    dp, bfly = lax.axis_index("dp"), lax.axis_index("bfly")
    core, y, xl = dp % 2, (dp // 2) % NY, dp // (2 * NY)
    z, xh = bfly // 2, bfly % 2
    z_dev = (dp, ((z + NZ // 2) % NZ) * 2 + xh)
    xh_dev = (dp, z * 2 + (1 - xh))
    core_dev = (dp + 1 - 2 * core, bfly)
    xl_dev = (((1 - xl) * NY + y) * 2 + core, bfly)


    def y_dev(to):
        return ((xl * NY + to) * 2 + core, bfly)

    def remote(src, dst, ss, rs, dev):
        return pltpu.make_async_remote_copy(
            src_ref=src, dst_ref=dst, send_sem=ss, recv_sem=rs, device_id=dev, device_id_type=MESH
        )

    def cols(k):
        return pl.ds(k * size, size)

    half = NZ // 2
    low = z < half
    plane = [y_dev((y + j) % NY) for j in range(1, NY)] + [xh_dev, xl_dev, core_dev]
    known = plane + [(dp, ((z + j) % half) * 2 + xh) for j in range(1, half)]
    barrier = pltpu.get_barrier_semaphore()
    pl.semaphore_signal(barrier, inc=1, device_id=z_dev, device_id_type=MESH)

    @pl.when(low)
    def _():
        for dev in known:
            pl.semaphore_signal(barrier, inc=1, device_id=dev, device_id_type=MESH)

    load_g = [pltpu.make_async_copy(g_hbm.at[:, cols(k)], gv.at[k], load_sem.at[k]) for k in range(n_blk)]
    load_x = [
        pltpu.make_async_copy(x_hbm.at[:, cols(k)], xv.at[k], load_sem.at[n_blk + k]) for k in range(n_blk)
    ]
    load_wb = [pltpu.make_async_copy(wb_hbm.at[s], wbv.at[s], load_sem.at[2 * n_blk + s]) for s in range(2)]
    load_wa = [pltpu.make_async_copy(wa_hbm.at[s], wav.at[s], load_sem.at[2 * n_blk + 2 + s]) for s in range(2)]
    pl.semaphore_wait(barrier, jnp.where(low, 1 + len(known), 1))

    send_x = [remote(x_hbm.at[:, cols(k)], xp.at[k], x_ss.at[k], x_rs.at[k], z_dev) for k in range(n_blk)]
    send_p = [remote(ps.at[k], pr.at[k], p_ss.at[k], p_rs.at[k], xh_dev) for k in range(n_blk)]
    for c in send_x:
        c.start()
    load_wb[1].start()
    for c in load_g:
        c.start()
    for c in load_x:
        c.start()
    load_wa[0].start()
    load_wb[0].start()
    load_wa[1].start()
    @pl.when(low)
    def _():
        for dev in known:
            pl.semaphore_signal(told, inc=1, device_id=dev, device_id_type=MESH)

    load_wb[1].wait()
    for k in range(n_blk):
        load_g[k].wait()
        ps[k] = dot_nt(gv[k], wbv[1, k]).astype(BF16)

    @pl.when(jnp.logical_not(low))
    def _():
        pl.semaphore_wait(go, 1)

    for c in send_p:
        c.start()

    @pl.when(low)
    def _():
        pl.semaphore_wait(told, len(known))
        pl.semaphore_signal(go, inc=1, device_id=z_dev, device_id_type=MESH)

    send_h = [remote(hv.at[k], hp.at[k], h_ss.at[k], h_rs.at[k], xh_dev) for k in range(n_blk)]
    land_c = [cr.at[k] for k in range(n_blk - 1)] + [last]
    send_c = [remote(cs.at[k], land_c[k], c_ss.at[k], c_rs.at[k], z_dev) for k in range(n_blk)]
    send_m = [
        [
            remote(
                loc.at[k, pl.ds(2 * h, 2), :, :, 1 - core],
                sib.at[k, pl.ds(2 * h, 2)],
                m_ss.at[k, h],
                m_rs.at[k, h],
                core_dev,
            )
            for h in range(2)
        ]
        for k in range(n_blk)
    ]
    send_a, send_y = (
        [
            [
                remote(
                    src.at[k, (y + j) % NY],
                    dst.at[k, j - 1],
                    ss.at[k, j - 1],
                    rs.at[k, j - 1],
                    y_dev((y + j) % NY),
                )
                for j in range(1, NY)
            ]
            for k in range(n_blk)
        ]
        for src, dst, ss, rs in ((asend, arecv, a_ss, a_rs), (ysend, yrecv, y_ss, y_rs))
    )
    send_t = [remote(tsend.at[k], trecv.at[k], t_ss.at[k], t_rs.at[k], xl_dev) for k in range(n_blk)]
    send_f = [
        remote(asum.at[k, 1 - xl], frecv.at[k], f_ss.at[k], f_rs.at[k], xl_dev) for k in range(n_blk)
    ]

    hold = jnp.where(z == 7, 2, jnp.where(z == 5, 2, jnp.where(z == 4, 2, jnp.where(z == 2, 3, jnp.where(z == 0, 2, 1)))))

    def keep(k, m, value):
        loc[k, m] = value.reshape(loc.shape[2:])

    def first_factor(k):
        load_x[k].wait()
        if k == 0:
            load_wa[0].wait()
            load_wa[1].wait()
            load_wb[0].wait()
        dhf[...] = dot_nt(gv[k], wbv[0, k])
        uf[...] = dot_nn(xv[k], wav[0, k])
        send_x[k].wait_recv()
        uf[...] += dot_nn(xp[k], wav[1, k])
        send_p[k].wait_recv()

        def rows(i, _):
            at = pl.ds(pl.multiple_of(i * ROWS, ROWS), ROWS)
            u = uf[at, :]
            dh = dhf[at, :] + pr[k, at, :].astype(F32)
            phi = 0.5 + 0.5 * lax.erf(u * F32(0.5**0.5))
            dens = jnp.exp(u * u * F32(-0.5)) * F32(0.3989422804014327)
            hv[k, at, :] = (u * phi).astype(BF16)
            du[k, at, :] = (dh * (phi + u * dens)).astype(BF16)
            return 0

        lax.fori_loop(0, size // ROWS, rows, 0)
        send_h[k].start()
        cs[k] = dot_nt(du[k], wav[1, k]).astype(BF16)

        @pl.when(hold == k)
        def _():
            for c in send_c[: k + 1]:
                c.start()

        @pl.when(hold < k)
        def _():
            send_c[k].start()

        keep(k, 0, dot_tn(xv[k], du[k]))
        keep(k, 1, dot_tn(xp[k], du[k]))
        send_m[k][0].start()
        if k < n_blk - 1:
            own[k] = dot_nt(du[k], wav[0, k])
        else:
            ownv[...] = dot_nt(du[k], wav[0, k])

    def second_factor(k):
        keep(k, 2, dot_tn(hv[k], gv[k]))
        mine = dot_nn(hv[k], wbv[0, k])
        send_h[k].wait_recv()
        keep(k, 3, dot_tn(hp[k], gv[k]))
        send_m[k][1].start()
        outv[:, cols(k)] = (mine + dot_nn(hp[k], wbv[1, k])).astype(BF16)

    def merged(k, h, s, at):
        return jnp.concatenate(
            [loc[k, m, s, at, core] + sib[k, m, s, at] for m in (2 * h, 2 * h + 1)], axis=-2
        )

    def a_to_owners(k):
        send_m[k][0].wait_recv()
        halves = [merged(k, 0, s, slice(None)) for s in range(2)]
        asend[k] = jnp.concatenate(halves, axis=1).astype(BF16)
        for j in (4, 3, 5, 2, 6, 1, 7):
            send_a[k][j - 1].start()

    def a_sum(k):
        for j in range(1, NY):
            send_a[k][j - 1].wait_recv()
        total = jnp.concatenate([merged(k, 0, s, y) for s in range(2)], axis=0)
        for j in range(NY - 1):
            total = total + arecv[k, j].astype(F32)
        asum[k] = total.reshape(asum.shape[1:])
        send_f[k].start()

    def a_finish(k):
        send_f[k].wait_recv()
        put(k, gav, asum[k, xl] + frecv[k])

    def b_to_half(k):
        send_m[k][1].wait_recv()
        tsend[k] = merged(k, 1, 1 - xl, slice(None)).astype(BF16)
        send_t[k].start()

    def b_to_owners(k):
        send_t[k].wait_recv()
        ysend[k] = (merged(k, 1, xl, slice(None)) + trecv[k].astype(F32)).astype(BF16)
        for j in (4, 3, 5, 2, 6, 1, 7):
            send_y[k][j - 1].start()

    def b_finish(k):
        for j in range(1, NY):
            send_y[k][j - 1].wait_recv()
        total = merged(k, 1, xl, y) + trecv[k, y].astype(F32)
        for j in range(NY - 1):
            total = total + yrecv[k, j].astype(F32)
        put(k, gbv, total)

    def put(k, into, total):
        total = total * scale
        for m in range(2):
            for r in range(8):
                at = 8 * m + r
                into[r, m, pl.ds(k, 1), :] = total[at : at + 1, :]

    def finish_input(k):
        send_c[k].wait_recv()
        giv[:, cols(k)] = (own[k] + cr[k].astype(F32)).astype(BF16)

    first_factor(0)
    first_factor(1)
    a_to_owners(0)
    first_factor(2)
    a_to_owners(1)
    second_factor(0)
    a_to_owners(2)
    b_to_half(0)
    second_factor(1)
    first_factor(3)
    b_to_half(1)
    b_to_owners(0)
    a_to_owners(3)
    second_factor(2)
    b_to_half(2)
    b_to_owners(1)
    a_sum(0)
    second_factor(3)
    a_sum(1)
    a_finish(0)
    b_to_half(3)
    b_to_owners(2)
    a_sum(2)
    b_finish(0)
    a_finish(1)
    b_to_owners(3)
    a_sum(3)
    finish_input(0)
    b_finish(1)
    a_finish(2)
    finish_input(1)
    b_finish(2)
    a_finish(3)
    finish_input(2)
    b_finish(3)
    for k in range(n_blk):
        for c in [send_x[k], send_p[k], send_h[k], *send_m[k], *send_a[k], *send_y[k], send_t[k], send_f[k]]:
            c.wait_send()
    for c in send_c:
        c.wait_send()
    send_c[3].wait_recv()


def shards(n_dp, tokens, weight_a, weight_b, upstream):
    rows, width = tokens.shape
    n_blk, size = weight_a.shape[1], weight_a.shape[2]
    own_rows = size // n_dp
    scale = float((rows * n_dp) ** -0.5)
    results = (
        jax.ShapeDtypeStruct((rows, width), BF16),
        jax.ShapeDtypeStruct((rows, width), BF16),
        jax.ShapeDtypeStruct((own_rows, 2, n_blk, size), F32),
        jax.ShapeDtypeStruct((own_rows, 2, n_blk, size), F32),
    )
    anywhere = pl.BlockSpec(memory_space=pl.ANY)
    act = pltpu.VMEM((n_blk, rows, size), BF16)
    weights = pltpu.VMEM((2, n_blk, size, size), BF16)
    dma = pltpu.SemaphoreType.DMA
    made = pl.pallas_call(
        functools.partial(main_kernel, scale),
        out_shape=(
            pltpu.VMEM((rows, width), BF16),
            pltpu.VMEM((rows, width - size), BF16),
            pltpu.VMEM((own_rows, 2, n_blk, size), F32),
            pltpu.VMEM((own_rows, 2, n_blk, size), F32),
            pltpu.VMEM((rows, size), F32),
            pltpu.VMEM((rows, size), BF16),
        ),
        in_specs=[anywhere] * 4,
        out_specs=[pl.BlockSpec(memory_space=pltpu.VMEM)] * 6,
        scratch_shapes=[
            act,
            act,
            weights,
            weights,
            act,
            act,
            act,
            act,
            act,
            act,
            act,
            pltpu.VMEM((rows, size), F32),
            pltpu.VMEM((rows, size), F32),
            act,
            pltpu.VMEM((n_blk, rows, size), F32),
            pltpu.VMEM((n_blk, 4, 2, NY, 2, own_rows, size), F32),
            pltpu.VMEM((n_blk, 4, 2, NY, own_rows, size), F32),
            pltpu.VMEM((n_blk, NY, 4 * own_rows, size), BF16),
            pltpu.VMEM((n_blk, NY - 1, 4 * own_rows, size), BF16),
            pltpu.VMEM((n_blk, 2, 2 * own_rows, size), F32),
            pltpu.VMEM((n_blk, 2 * own_rows, size), F32),
            pltpu.VMEM((n_blk, NY, 2 * own_rows, size), BF16),
            pltpu.VMEM((n_blk, NY - 1, 2 * own_rows, size), BF16),
            pltpu.VMEM((n_blk, NY, 2 * own_rows, size), BF16),
            pltpu.VMEM((n_blk, NY, 2 * own_rows, size), BF16),
            dma((2 * n_blk + 4,)),
            dma((n_blk,)),
            dma((n_blk,)),
            dma((n_blk,)),
            dma((n_blk,)),
            dma((n_blk,)),
            dma((n_blk,)),
            dma((n_blk,)),
            dma((n_blk,)),
            dma((n_blk, 2)),
            dma((n_blk, 2)),
            dma((n_blk, NY - 1)),
            dma((n_blk, NY - 1)),
            dma((n_blk,)),
            dma((n_blk,)),
            dma((n_blk, NY - 1)),
            dma((n_blk, NY - 1)),
            dma((n_blk,)),
            dma((n_blk,)),
            pltpu.SemaphoreType.REGULAR,
            pltpu.SemaphoreType.REGULAR,
        ],
        compiler_params=pltpu.CompilerParams(
            collective_id=0, has_side_effects=True, vmem_limit_bytes=40 << 20
        ),
    )(*[pltpu.with_memory_space_constraint(a, pltpu.HBM) for a in (tokens, upstream, weight_a, weight_b)])
    return pl.pallas_call(
        copy_kernel,
        out_shape=results,
        in_specs=[anywhere] * 4 + [pl.BlockSpec(memory_space=pltpu.VMEM)] * 2,
        out_specs=[anywhere] * 4,
        scratch_shapes=[pltpu.VMEM((rows, size), BF16), dma((5,))],
    )(*[pltpu.with_memory_space_constraint(a, pltpu.VMEM) for a in made])


def copy_kernel(out, gi, ga, gb, own, last, out_to, gi_to, ga_to, gb_to, block, sems):
    done = gi.shape[1]
    copies = [
        pltpu.make_async_copy(out, out_to, sems.at[0]),
        pltpu.make_async_copy(gi, gi_to.at[:, pl.ds(0, done)], sems.at[1]),
        pltpu.make_async_copy(ga, ga_to, sems.at[2]),
        pltpu.make_async_copy(gb, gb_to, sems.at[3]),
        pltpu.make_async_copy(block, gi_to.at[:, pl.ds(done, block.shape[1])], sems.at[4]),
    ]
    for c in copies[:4]:
        c.start()
    block[...] = (own[...] + last[...].astype(F32)).astype(BF16)
    copies[4].start()
    for c in copies:
        c.wait()


def solution(mesh):
    in_specs = (
        P("dp", "bfly"),
        P(None, "bfly", None, None),
        P(None, "bfly", None, None),
        P("dp", "bfly"),
    )
    out_specs = (
        P("dp", "bfly"),
        P("dp", "bfly"),
        P("dp", None, "bfly", None),
        P("dp", None, "bfly", None),
    )
    return jax.shard_map(
        functools.partial(shards, mesh.shape["dp"]),
        mesh=mesh,
        in_specs=in_specs,
        out_specs=out_specs,
        check_vma=False,
    )
```

```python
import functools

import jax
import jax.numpy as jnp
from jax import lax
from jax.experimental import pallas as pl
from jax.experimental.pallas import tpu as pltpu
from jax.sharding import PartitionSpec as P

MESH = pl.DeviceIdType.MESH
NY = 8
NZ = 8
F32 = jnp.float32
BF16 = jnp.bfloat16
ROWS = 32


def dot_nn(a, b):
    return lax.dot_general(a, b, (((1,), (0,)), ((), ())), preferred_element_type=F32)


def dot_nt(a, b):
    return lax.dot_general(a, b, (((1,), (1,)), ((), ())), preferred_element_type=F32)


def dot_tn(a, b):
    return lax.dot_general(a, b, (((0,), (0,)), ((), ())), preferred_element_type=F32)


def main_kernel(
    scale,
    x_hbm,
    g_hbm,
    wa_hbm,
    wb_hbm,
    outv,
    giv,
    gav,
    gbv,
    ownv,
    last,
    xv,
    gv,
    wav,
    wbv,
    xp,
    ps,
    pr,
    hv,
    hp,
    cs,
    cr,
    uf,
    dhf,
    du,
    own,
    loc,
    sib,
    asend,
    arecv,
    asum,
    frecv,
    ysend,
    yrecv,
    tsend,
    trecv,
    load_sem,
    x_ss,
    x_rs,
    p_ss,
    p_rs,
    h_ss,
    h_rs,
    c_ss,
    c_rs,
    m_ss,
    m_rs,
    a_ss,
    a_rs,
    f_ss,
    f_rs,
    y_ss,
    y_rs,
    t_ss,
    t_rs,
    told,
    go,
    told_x,
    go_x,
):
    n_blk, size = xv.shape[0], xv.shape[1]
    dp, bfly = lax.axis_index("dp"), lax.axis_index("bfly")
    core, y, xl = dp % 2, (dp // 2) % NY, dp // (2 * NY)
    z, xh = bfly // 2, bfly % 2
    z_dev = (dp, ((z + NZ // 2) % NZ) * 2 + xh)
    xh_dev = (dp, z * 2 + (1 - xh))
    core_dev = (dp + 1 - 2 * core, bfly)
    xl_dev = (((1 - xl) * NY + y) * 2 + core, bfly)


    def y_dev(to):
        return ((xl * NY + to) * 2 + core, bfly)

    def remote(src, dst, ss, rs, dev):
        return pltpu.make_async_remote_copy(
            src_ref=src, dst_ref=dst, send_sem=ss, recv_sem=rs, device_id=dev, device_id_type=MESH
        )

    def cols(k):
        return pl.ds(k * size, size)

    half = NZ // 2
    low = z < half
    plane = [y_dev((y + j) % NY) for j in range(1, NY)] + [xh_dev, xl_dev, core_dev]
    known = plane + [(dp, ((z + j) % half) * 2 + xh) for j in range(1, half)]
    barrier = pltpu.get_barrier_semaphore()
    pl.semaphore_signal(barrier, inc=1, device_id=z_dev, device_id_type=MESH)

    @pl.when(low)
    def _():
        for dev in known:
            pl.semaphore_signal(barrier, inc=1, device_id=dev, device_id_type=MESH)

    load_g = [pltpu.make_async_copy(g_hbm.at[:, cols(k)], gv.at[k], load_sem.at[k]) for k in range(n_blk)]
    load_x = [
        pltpu.make_async_copy(x_hbm.at[:, cols(k)], xv.at[k], load_sem.at[n_blk + k]) for k in range(n_blk)
    ]
    load_wb = [pltpu.make_async_copy(wb_hbm.at[s], wbv.at[s], load_sem.at[2 * n_blk + s]) for s in range(2)]
    load_wa = [pltpu.make_async_copy(wa_hbm.at[s], wav.at[s], load_sem.at[2 * n_blk + 2 + s]) for s in range(2)]
    pl.semaphore_wait(barrier, jnp.where(low, 1 + len(known), 1))

    send_x = [remote(x_hbm.at[:, cols(k)], xp.at[k], x_ss.at[k], x_rs.at[k], z_dev) for k in range(n_blk)]
    send_p = [remote(ps.at[k], pr.at[k], p_ss.at[k], p_rs.at[k], xh_dev) for k in range(n_blk)]
    for c in send_x:
        c.start()
    load_wb[1].start()
    for c in load_g:
        c.start()
    for c in load_x:
        c.start()
    load_wa[0].start()
    load_wb[0].start()
    load_wa[1].start()
    @pl.when(low)
    def _():
        pl.semaphore_signal(told_x, inc=1, device_id=xh_dev, device_id_type=MESH)
        for dev in known:
            pl.semaphore_signal(told, inc=1, device_id=dev, device_id_type=MESH)
        pl.semaphore_wait(told_x, 1)
        pl.semaphore_signal(go_x, inc=1, device_id=z_dev, device_id_type=MESH)

    load_wb[1].wait()
    for k in range(n_blk):
        load_g[k].wait()
        ps[k] = dot_nt(gv[k], wbv[1, k]).astype(BF16)

    @pl.when(jnp.logical_not(low))
    def _():
        pl.semaphore_wait(go_x, 1)

    for c in send_p:
        c.start()

    @pl.when(low)
    def _():
        pl.semaphore_wait(told, len(known))
        pl.semaphore_signal(go, inc=1, device_id=z_dev, device_id_type=MESH)

    @pl.when(jnp.logical_not(low))
    def _():
        pl.semaphore_wait(go, 1)

    send_h = [remote(hv.at[k], hp.at[k], h_ss.at[k], h_rs.at[k], xh_dev) for k in range(n_blk)]
    land_c = [cr.at[k] for k in range(n_blk - 1)] + [last]
    send_c = [remote(cs.at[k], land_c[k], c_ss.at[k], c_rs.at[k], z_dev) for k in range(n_blk)]
    send_m = [
        [
            remote(
                loc.at[k, pl.ds(2 * h, 2), :, :, 1 - core],
                sib.at[k, pl.ds(2 * h, 2)],
                m_ss.at[k, h],
                m_rs.at[k, h],
                core_dev,
            )
            for h in range(2)
        ]
        for k in range(n_blk)
    ]
    send_a, send_y = (
        [
            [
                remote(
                    src.at[k, (y + j) % NY],
                    dst.at[k, j - 1],
                    ss.at[k, j - 1],
                    rs.at[k, j - 1],
                    y_dev((y + j) % NY),
                )
                for j in range(1, NY)
            ]
            for k in range(n_blk)
        ]
        for src, dst, ss, rs in ((asend, arecv, a_ss, a_rs), (ysend, yrecv, y_ss, y_rs))
    )
    send_t = [remote(tsend.at[k], trecv.at[k], t_ss.at[k], t_rs.at[k], xl_dev) for k in range(n_blk)]
    send_f = [
        remote(asum.at[k, 1 - xl], frecv.at[k], f_ss.at[k], f_rs.at[k], xl_dev) for k in range(n_blk)
    ]

    hold = jnp.where(z == 7, 2, jnp.where(z == 5, 2, jnp.where(z == 4, 2, jnp.where(z == 2, 3, jnp.where(z == 0, 2, 1)))))

    def keep(k, m, value):
        loc[k, m] = value.reshape(loc.shape[2:])

    def first_factor(k):
        load_x[k].wait()
        if k == 0:
            load_wa[0].wait()
            load_wa[1].wait()
            load_wb[0].wait()
        dhf[...] = dot_nt(gv[k], wbv[0, k])
        uf[...] = dot_nn(xv[k], wav[0, k])
        send_x[k].wait_recv()
        uf[...] += dot_nn(xp[k], wav[1, k])
        send_p[k].wait_recv()

        def rows(i, _):
            at = pl.ds(pl.multiple_of(i * ROWS, ROWS), ROWS)
            u = uf[at, :]
            dh = dhf[at, :] + pr[k, at, :].astype(F32)
            phi = 0.5 + 0.5 * lax.erf(u * F32(0.5**0.5))
            dens = jnp.exp(u * u * F32(-0.5)) * F32(0.3989422804014327)
            hv[k, at, :] = (u * phi).astype(BF16)
            du[k, at, :] = (dh * (phi + u * dens)).astype(BF16)
            return 0

        lax.fori_loop(0, size // ROWS, rows, 0)
        send_h[k].start()
        cs[k] = dot_nt(du[k], wav[1, k]).astype(BF16)

        @pl.when(hold == k)
        def _():
            for c in send_c[: k + 1]:
                c.start()

        @pl.when(hold < k)
        def _():
            send_c[k].start()

        keep(k, 0, dot_tn(xv[k], du[k]))
        keep(k, 1, dot_tn(xp[k], du[k]))
        send_m[k][0].start()
        if k < n_blk - 1:
            own[k] = dot_nt(du[k], wav[0, k])
        else:
            ownv[...] = dot_nt(du[k], wav[0, k])

    def second_factor(k):
        keep(k, 2, dot_tn(hv[k], gv[k]))
        mine = dot_nn(hv[k], wbv[0, k])
        send_h[k].wait_recv()
        keep(k, 3, dot_tn(hp[k], gv[k]))
        send_m[k][1].start()
        outv[:, cols(k)] = (mine + dot_nn(hp[k], wbv[1, k])).astype(BF16)

    def merged(k, h, s, at):
        return jnp.concatenate(
            [loc[k, m, s, at, core] + sib[k, m, s, at] for m in (2 * h, 2 * h + 1)], axis=-2
        )

    def a_to_owners(k):
        send_m[k][0].wait_recv()
        halves = [merged(k, 0, s, slice(None)) for s in range(2)]
        asend[k] = jnp.concatenate(halves, axis=1).astype(BF16)
        for j in (4, 3, 5, 2, 6, 1, 7):
            send_a[k][j - 1].start()

    def a_sum(k):
        for j in range(1, NY):
            send_a[k][j - 1].wait_recv()
        total = jnp.concatenate([merged(k, 0, s, y) for s in range(2)], axis=0)
        for j in range(NY - 1):
            total = total + arecv[k, j].astype(F32)
        asum[k] = total.reshape(asum.shape[1:])
        send_f[k].start()

    def a_finish(k):
        send_f[k].wait_recv()
        put(k, gav, asum[k, xl] + frecv[k])

    def b_to_half(k):
        send_m[k][1].wait_recv()
        tsend[k] = merged(k, 1, 1 - xl, slice(None)).astype(BF16)
        send_t[k].start()

    def b_to_owners(k):
        send_t[k].wait_recv()
        ysend[k] = (merged(k, 1, xl, slice(None)) + trecv[k].astype(F32)).astype(BF16)
        for j in (4, 3, 5, 2, 6, 1, 7):
            send_y[k][j - 1].start()

    def b_finish(k):
        for j in range(1, NY):
            send_y[k][j - 1].wait_recv()
        total = merged(k, 1, xl, y) + trecv[k, y].astype(F32)
        for j in range(NY - 1):
            total = total + yrecv[k, j].astype(F32)
        put(k, gbv, total)

    def put(k, into, total):
        total = total * scale
        for m in range(2):
            for r in range(8):
                at = 8 * m + r
                into[r, m, pl.ds(k, 1), :] = total[at : at + 1, :]

    def finish_input(k):
        send_c[k].wait_recv()
        giv[:, cols(k)] = (own[k] + cr[k].astype(F32)).astype(BF16)

    first_factor(0)
    first_factor(1)
    a_to_owners(0)
    first_factor(2)
    a_to_owners(1)
    second_factor(0)
    a_to_owners(2)
    b_to_half(0)
    second_factor(1)
    first_factor(3)
    b_to_half(1)
    b_to_owners(0)
    a_to_owners(3)
    second_factor(2)
    b_to_half(2)
    b_to_owners(1)
    a_sum(0)
    second_factor(3)
    a_sum(1)
    a_finish(0)
    b_to_half(3)
    b_to_owners(2)
    a_sum(2)
    b_finish(0)
    a_finish(1)
    b_to_owners(3)
    a_sum(3)
    finish_input(0)
    b_finish(1)
    a_finish(2)
    finish_input(1)
    b_finish(2)
    a_finish(3)
    finish_input(2)
    b_finish(3)
    for k in range(n_blk):
        for c in [send_x[k], send_p[k], send_h[k], *send_m[k], *send_a[k], *send_y[k], send_t[k], send_f[k]]:
            c.wait_send()
    for c in send_c:
        c.wait_send()
    send_c[3].wait_recv()


def shards(n_dp, tokens, weight_a, weight_b, upstream):
    rows, width = tokens.shape
    n_blk, size = weight_a.shape[1], weight_a.shape[2]
    own_rows = size // n_dp
    scale = float((rows * n_dp) ** -0.5)
    results = (
        jax.ShapeDtypeStruct((rows, width), BF16),
        jax.ShapeDtypeStruct((rows, width), BF16),
        jax.ShapeDtypeStruct((own_rows, 2, n_blk, size), F32),
        jax.ShapeDtypeStruct((own_rows, 2, n_blk, size), F32),
    )
    anywhere = pl.BlockSpec(memory_space=pl.ANY)
    act = pltpu.VMEM((n_blk, rows, size), BF16)
    weights = pltpu.VMEM((2, n_blk, size, size), BF16)
    dma = pltpu.SemaphoreType.DMA
    made = pl.pallas_call(
        functools.partial(main_kernel, scale),
        out_shape=(
            pltpu.VMEM((rows, width), BF16),
            pltpu.VMEM((rows, width - size), BF16),
            pltpu.VMEM((own_rows, 2, n_blk, size), F32),
            pltpu.VMEM((own_rows, 2, n_blk, size), F32),
            pltpu.VMEM((rows, size), F32),
            pltpu.VMEM((rows, size), BF16),
        ),
        in_specs=[anywhere] * 4,
        out_specs=[pl.BlockSpec(memory_space=pltpu.VMEM)] * 6,
        scratch_shapes=[
            act,
            act,
            weights,
            weights,
            act,
            act,
            act,
            act,
            act,
            act,
            act,
            pltpu.VMEM((rows, size), F32),
            pltpu.VMEM((rows, size), F32),
            act,
            pltpu.VMEM((n_blk, rows, size), F32),
            pltpu.VMEM((n_blk, 4, 2, NY, 2, own_rows, size), F32),
            pltpu.VMEM((n_blk, 4, 2, NY, own_rows, size), F32),
            pltpu.VMEM((n_blk, NY, 4 * own_rows, size), BF16),
            pltpu.VMEM((n_blk, NY - 1, 4 * own_rows, size), BF16),
            pltpu.VMEM((n_blk, 2, 2 * own_rows, size), F32),
            pltpu.VMEM((n_blk, 2 * own_rows, size), F32),
            pltpu.VMEM((n_blk, NY, 2 * own_rows, size), BF16),
            pltpu.VMEM((n_blk, NY - 1, 2 * own_rows, size), BF16),
            pltpu.VMEM((n_blk, NY, 2 * own_rows, size), BF16),
            pltpu.VMEM((n_blk, NY, 2 * own_rows, size), BF16),
            dma((2 * n_blk + 4,)),
            dma((n_blk,)),
            dma((n_blk,)),
            dma((n_blk,)),
            dma((n_blk,)),
            dma((n_blk,)),
            dma((n_blk,)),
            dma((n_blk,)),
            dma((n_blk,)),
            dma((n_blk, 2)),
            dma((n_blk, 2)),
            dma((n_blk, NY - 1)),
            dma((n_blk, NY - 1)),
            dma((n_blk,)),
            dma((n_blk,)),
            dma((n_blk, NY - 1)),
            dma((n_blk, NY - 1)),
            dma((n_blk,)),
            dma((n_blk,)),
            pltpu.SemaphoreType.REGULAR,
            pltpu.SemaphoreType.REGULAR,
            pltpu.SemaphoreType.REGULAR,
            pltpu.SemaphoreType.REGULAR,
        ],
        compiler_params=pltpu.CompilerParams(
            collective_id=0, has_side_effects=True, vmem_limit_bytes=40 << 20
        ),
    )(*[pltpu.with_memory_space_constraint(a, pltpu.HBM) for a in (tokens, upstream, weight_a, weight_b)])
    return pl.pallas_call(
        copy_kernel,
        out_shape=results,
        in_specs=[anywhere] * 4 + [pl.BlockSpec(memory_space=pltpu.VMEM)] * 2,
        out_specs=[anywhere] * 4,
        scratch_shapes=[pltpu.VMEM((rows, size), BF16), dma((5,))],
    )(*[pltpu.with_memory_space_constraint(a, pltpu.VMEM) for a in made])


def copy_kernel(out, gi, ga, gb, own, last, out_to, gi_to, ga_to, gb_to, block, sems):
    done = gi.shape[1]
    copies = [
        pltpu.make_async_copy(out, out_to, sems.at[0]),
        pltpu.make_async_copy(gi, gi_to.at[:, pl.ds(0, done)], sems.at[1]),
        pltpu.make_async_copy(ga, ga_to, sems.at[2]),
        pltpu.make_async_copy(gb, gb_to, sems.at[3]),
        pltpu.make_async_copy(block, gi_to.at[:, pl.ds(done, block.shape[1])], sems.at[4]),
    ]
    for c in copies[:4]:
        c.start()
    block[...] = (own[...] + last[...].astype(F32)).astype(BF16)
    copies[4].start()
    for c in copies:
        c.wait()


def solution(mesh):
    in_specs = (
        P("dp", "bfly"),
        P(None, "bfly", None, None),
        P(None, "bfly", None, None),
        P("dp", "bfly"),
    )
    out_specs = (
        P("dp", "bfly"),
        P("dp", "bfly"),
        P("dp", None, "bfly", None),
        P("dp", None, "bfly", None),
    )
    return jax.shard_map(
        functools.partial(shards, mesh.shape["dp"]),
        mesh=mesh,
        in_specs=in_specs,
        out_specs=out_specs,
        check_vma=False,
    )
```

```python
import functools

import jax
import jax.numpy as jnp
from jax import lax
from jax.experimental import pallas as pl
from jax.experimental.pallas import tpu as pltpu
from jax.sharding import PartitionSpec as P

MESH = pl.DeviceIdType.MESH
NY = 8
NZ = 8
F32 = jnp.float32
BF16 = jnp.bfloat16
ROWS = 32


def dot_nn(a, b):
    return lax.dot_general(a, b, (((1,), (0,)), ((), ())), preferred_element_type=F32)


def dot_nt(a, b):
    return lax.dot_general(a, b, (((1,), (1,)), ((), ())), preferred_element_type=F32)


def dot_tn(a, b):
    return lax.dot_general(a, b, (((0,), (0,)), ((), ())), preferred_element_type=F32)


def main_kernel(
    scale,
    x_hbm,
    g_hbm,
    wa_hbm,
    wb_hbm,
    outv,
    giv,
    gav,
    gbv,
    ownv,
    last,
    xv,
    gv,
    wav,
    wbv,
    xp,
    ps,
    pr,
    hv,
    hp,
    cs,
    cr,
    uf,
    dhf,
    du,
    own,
    loc,
    sib,
    asend,
    arecv,
    asum,
    frecv,
    ysend,
    yrecv,
    tsend,
    trecv,
    load_sem,
    x_ss,
    x_rs,
    p_ss,
    p_rs,
    h_ss,
    h_rs,
    c_ss,
    c_rs,
    m_ss,
    m_rs,
    a_ss,
    a_rs,
    f_ss,
    f_rs,
    y_ss,
    y_rs,
    t_ss,
    t_rs,
    told,
    go,
    told_x,
    go_x,
):
    n_blk, size = xv.shape[0], xv.shape[1]
    dp, bfly = lax.axis_index("dp"), lax.axis_index("bfly")
    core, y, xl = dp % 2, (dp // 2) % NY, dp // (2 * NY)
    z, xh = bfly // 2, bfly % 2
    z_dev = (dp, ((z + NZ // 2) % NZ) * 2 + xh)
    xh_dev = (dp, z * 2 + (1 - xh))
    core_dev = (dp + 1 - 2 * core, bfly)
    xl_dev = (((1 - xl) * NY + y) * 2 + core, bfly)


    def y_dev(to):
        return ((xl * NY + to) * 2 + core, bfly)

    def remote(src, dst, ss, rs, dev):
        return pltpu.make_async_remote_copy(
            src_ref=src, dst_ref=dst, send_sem=ss, recv_sem=rs, device_id=dev, device_id_type=MESH
        )

    def cols(k):
        return pl.ds(k * size, size)

    half = NZ // 2
    low = z < half
    plane = [y_dev((y + j) % NY) for j in range(1, NY)] + [xh_dev, xl_dev, core_dev]
    known = plane + [(dp, ((z + j) % half) * 2 + xh) for j in range(1, half)]
    barrier = pltpu.get_barrier_semaphore()
    pl.semaphore_signal(barrier, inc=1, device_id=z_dev, device_id_type=MESH)

    @pl.when(low)
    def _():
        for dev in known:
            pl.semaphore_signal(barrier, inc=1, device_id=dev, device_id_type=MESH)

    load_g = [pltpu.make_async_copy(g_hbm.at[:, cols(k)], gv.at[k], load_sem.at[k]) for k in range(n_blk)]
    load_x = [
        pltpu.make_async_copy(x_hbm.at[:, cols(k)], xv.at[k], load_sem.at[n_blk + k]) for k in range(n_blk)
    ]
    load_wb = [pltpu.make_async_copy(wb_hbm.at[s], wbv.at[s], load_sem.at[2 * n_blk + s]) for s in range(2)]
    load_wa = [pltpu.make_async_copy(wa_hbm.at[s], wav.at[s], load_sem.at[2 * n_blk + 2 + s]) for s in range(2)]
    pl.semaphore_wait(barrier, jnp.where(low, 1 + len(known), 1))

    send_x = [remote(x_hbm.at[:, cols(k)], xp.at[k], x_ss.at[k], x_rs.at[k], z_dev) for k in range(n_blk)]
    send_p = [remote(ps.at[k], pr.at[k], p_ss.at[k], p_rs.at[k], xh_dev) for k in range(n_blk)]
    for c in send_x:
        c.start()
    load_wb[1].start()
    for c in load_g:
        c.start()
    for c in load_x:
        c.start()
    load_wa[0].start()
    load_wb[0].start()
    load_wa[1].start()
    @pl.when(low)
    def _():
        pl.semaphore_signal(told_x, inc=1, device_id=xh_dev, device_id_type=MESH)
        for dev in known:
            pl.semaphore_signal(told, inc=1, device_id=dev, device_id_type=MESH)
        pl.semaphore_wait(told_x, 1)
        pl.semaphore_signal(go_x, inc=1, device_id=z_dev, device_id_type=MESH)

    load_wb[1].wait()
    for k in range(n_blk):
        load_g[k].wait()
        ps[k] = dot_nt(gv[k], wbv[1, k]).astype(BF16)

    @pl.when(jnp.logical_not(low))
    def _():
        pl.semaphore_wait(go_x, 1)

    for c in send_p:
        c.start()

    @pl.when(low)
    def _():
        pl.semaphore_wait(told, len(known))
        pl.semaphore_signal(go, inc=1, device_id=z_dev, device_id_type=MESH)

    @pl.when(jnp.logical_not(low))
    def _():
        pl.semaphore_wait(go, 1)

    send_h = [remote(hv.at[k], hp.at[k], h_ss.at[k], h_rs.at[k], xh_dev) for k in range(n_blk)]
    land_c = [cr.at[k] for k in range(n_blk - 1)] + [last]
    send_c = [remote(cs.at[k], land_c[k], c_ss.at[k], c_rs.at[k], z_dev) for k in range(n_blk)]
    send_m = [
        [
            remote(
                loc.at[k, pl.ds(2 * h, 2), :, :, 1 - core],
                sib.at[k, pl.ds(2 * h, 2)],
                m_ss.at[k, h],
                m_rs.at[k, h],
                core_dev,
            )
            for h in range(2)
        ]
        for k in range(n_blk)
    ]
    send_a, send_y = (
        [
            [
                remote(
                    src.at[k, (y + j) % NY],
                    dst.at[k, j - 1],
                    ss.at[k, j - 1],
                    rs.at[k, j - 1],
                    y_dev((y + j) % NY),
                )
                for j in range(1, NY)
            ]
            for k in range(n_blk)
        ]
        for src, dst, ss, rs in ((asend, arecv, a_ss, a_rs), (ysend, yrecv, y_ss, y_rs))
    )
    send_t = [remote(tsend.at[k], trecv.at[k], t_ss.at[k], t_rs.at[k], xl_dev) for k in range(n_blk)]
    send_f = [
        remote(asum.at[k, 1 - xl], frecv.at[k], f_ss.at[k], f_rs.at[k], xl_dev) for k in range(n_blk)
    ]

    hold = jnp.where(z == 7, 2, jnp.where(z == 5, 2, jnp.where(z == 4, 2, jnp.where(z == 2, 3, jnp.where(z == 0, 2, 1)))))

    def keep(k, m, value):
        loc[k, m] = value.reshape(loc.shape[2:])

    def first_factor(k):
        load_x[k].wait()
        if k == 0:
            load_wa[0].wait()
            load_wa[1].wait()
            load_wb[0].wait()
        dhf[...] = dot_nt(gv[k], wbv[0, k])
        uf[...] = dot_nn(xv[k], wav[0, k])
        send_x[k].wait_recv()
        uf[...] += dot_nn(xp[k], wav[1, k])
        send_p[k].wait_recv()

        def rows(i, _):
            at = pl.ds(pl.multiple_of(i * ROWS, ROWS), ROWS)
            u = uf[at, :]
            dh = dhf[at, :] + pr[k, at, :].astype(F32)
            phi = 0.5 + 0.5 * lax.erf(u * F32(0.5**0.5))
            dens = jnp.exp(u * u * F32(-0.5)) * F32(0.3989422804014327)
            hv[k, at, :] = (u * phi).astype(BF16)
            du[k, at, :] = (dh * (phi + u * dens)).astype(BF16)
            return 0

        lax.fori_loop(0, size // ROWS, rows, 0)
        send_h[k].start()
        cs[k] = dot_nt(du[k], wav[1, k]).astype(BF16)

        @pl.when(hold == k)
        def _():
            for c in send_c[: k + 1]:
                c.start()

        @pl.when(hold < k)
        def _():
            send_c[k].start()

        keep(k, 0, dot_tn(xv[k], du[k]))
        keep(k, 1, dot_tn(xp[k], du[k]))
        send_m[k][0].start()
        if k < n_blk - 1:
            own[k] = dot_nt(du[k], wav[0, k])
        else:
            ownv[...] = dot_nt(du[k], wav[0, k])

    def second_factor(k):
        keep(k, 2, dot_tn(hv[k], gv[k]))
        mine = dot_nn(hv[k], wbv[0, k])
        send_h[k].wait_recv()
        keep(k, 3, dot_tn(hp[k], gv[k]))
        send_m[k][1].start()
        outv[:, cols(k)] = (mine + dot_nn(hp[k], wbv[1, k])).astype(BF16)

    def merged(k, h, s, at):
        return jnp.concatenate(
            [loc[k, m, s, at, core] + sib[k, m, s, at] for m in (2 * h, 2 * h + 1)], axis=-2
        )

    def a_to_owners(k):
        send_m[k][0].wait_recv()
        halves = [merged(k, 0, s, slice(None)) for s in range(2)]
        asend[k] = jnp.concatenate(halves, axis=1).astype(BF16)
        for j in (4, 3, 5, 2, 6, 1, 7):
            send_a[k][j - 1].start()

    def a_sum(k):
        for j in range(1, NY):
            send_a[k][j - 1].wait_recv()
        total = jnp.concatenate([merged(k, 0, s, y) for s in range(2)], axis=0)
        for j in range(NY - 1):
            total = total + arecv[k, j].astype(F32)
        asum[k] = total.reshape(asum.shape[1:])
        send_f[k].start()

    def a_finish(k):
        send_f[k].wait_recv()
        put(k, gav, asum[k, xl] + frecv[k])

    def b_to_half(k):
        send_m[k][1].wait_recv()
        tsend[k] = merged(k, 1, 1 - xl, slice(None)).astype(BF16)
        send_t[k].start()

    def b_to_owners(k):
        send_t[k].wait_recv()
        ysend[k] = (merged(k, 1, xl, slice(None)) + trecv[k].astype(F32)).astype(BF16)
        for j in (4, 3, 5, 2, 6, 1, 7):
            send_y[k][j - 1].start()

    def b_finish(k):
        for j in range(1, NY):
            send_y[k][j - 1].wait_recv()
        total = merged(k, 1, xl, y) + trecv[k, y].astype(F32)
        for j in range(NY - 1):
            total = total + yrecv[k, j].astype(F32)
        put(k, gbv, total)

    def put(k, into, total):
        total = total * scale
        for m in range(2):
            for r in range(8):
                at = 8 * m + r
                into[r, m, pl.ds(k, 1), :] = total[at : at + 1, :]

    def finish_input(k):
        send_c[k].wait_recv()
        giv[:, cols(k)] = (own[k] + cr[k].astype(F32)).astype(BF16)

    first_factor(0)
    first_factor(1)
    a_to_owners(0)
    first_factor(2)
    a_to_owners(1)
    second_factor(0)
    a_to_owners(2)
    b_to_half(0)
    second_factor(1)
    first_factor(3)
    b_to_half(1)
    b_to_owners(0)
    a_to_owners(3)
    second_factor(2)
    b_to_half(2)
    b_to_owners(1)
    a_sum(0)
    second_factor(3)
    a_sum(1)
    a_finish(0)
    b_to_half(3)
    finish_input(0)
    b_to_owners(2)
    a_sum(2)
    b_finish(0)
    a_finish(1)
    b_to_owners(3)
    a_sum(3)
    finish_input(1)
    b_finish(1)
    a_finish(2)
    b_finish(2)
    a_finish(3)
    finish_input(2)
    b_finish(3)
    for k in range(n_blk):
        for c in [send_x[k], send_p[k], send_h[k], *send_m[k], *send_a[k], *send_y[k], send_t[k], send_f[k]]:
            c.wait_send()
    for c in send_c:
        c.wait_send()
    send_c[3].wait_recv()


def shards(n_dp, tokens, weight_a, weight_b, upstream):
    rows, width = tokens.shape
    n_blk, size = weight_a.shape[1], weight_a.shape[2]
    own_rows = size // n_dp
    scale = float((rows * n_dp) ** -0.5)
    results = (
        jax.ShapeDtypeStruct((rows, width), BF16),
        jax.ShapeDtypeStruct((rows, width), BF16),
        jax.ShapeDtypeStruct((own_rows, 2, n_blk, size), F32),
        jax.ShapeDtypeStruct((own_rows, 2, n_blk, size), F32),
    )
    anywhere = pl.BlockSpec(memory_space=pl.ANY)
    act = pltpu.VMEM((n_blk, rows, size), BF16)
    weights = pltpu.VMEM((2, n_blk, size, size), BF16)
    dma = pltpu.SemaphoreType.DMA
    made = pl.pallas_call(
        functools.partial(main_kernel, scale),
        out_shape=(
            pltpu.VMEM((rows, width), BF16),
            pltpu.VMEM((rows, width - size), BF16),
            pltpu.VMEM((own_rows, 2, n_blk, size), F32),
            pltpu.VMEM((own_rows, 2, n_blk, size), F32),
            pltpu.VMEM((rows, size), F32),
            pltpu.VMEM((rows, size), BF16),
        ),
        in_specs=[anywhere] * 4,
        out_specs=[pl.BlockSpec(memory_space=pltpu.VMEM)] * 6,
        scratch_shapes=[
            act,
            act,
            weights,
            weights,
            act,
            act,
            act,
            act,
            act,
            act,
            act,
            pltpu.VMEM((rows, size), F32),
            pltpu.VMEM((rows, size), F32),
            act,
            pltpu.VMEM((n_blk, rows, size), F32),
            pltpu.VMEM((n_blk, 4, 2, NY, 2, own_rows, size), F32),
            pltpu.VMEM((n_blk, 4, 2, NY, own_rows, size), F32),
            pltpu.VMEM((n_blk, NY, 4 * own_rows, size), BF16),
            pltpu.VMEM((n_blk, NY - 1, 4 * own_rows, size), BF16),
            pltpu.VMEM((n_blk, 2, 2 * own_rows, size), F32),
            pltpu.VMEM((n_blk, 2 * own_rows, size), F32),
            pltpu.VMEM((n_blk, NY, 2 * own_rows, size), BF16),
            pltpu.VMEM((n_blk, NY - 1, 2 * own_rows, size), BF16),
            pltpu.VMEM((n_blk, NY, 2 * own_rows, size), BF16),
            pltpu.VMEM((n_blk, NY, 2 * own_rows, size), BF16),
            dma((2 * n_blk + 4,)),
            dma((n_blk,)),
            dma((n_blk,)),
            dma((n_blk,)),
            dma((n_blk,)),
            dma((n_blk,)),
            dma((n_blk,)),
            dma((n_blk,)),
            dma((n_blk,)),
            dma((n_blk, 2)),
            dma((n_blk, 2)),
            dma((n_blk, NY - 1)),
            dma((n_blk, NY - 1)),
            dma((n_blk,)),
            dma((n_blk,)),
            dma((n_blk, NY - 1)),
            dma((n_blk, NY - 1)),
            dma((n_blk,)),
            dma((n_blk,)),
            pltpu.SemaphoreType.REGULAR,
            pltpu.SemaphoreType.REGULAR,
            pltpu.SemaphoreType.REGULAR,
            pltpu.SemaphoreType.REGULAR,
        ],
        compiler_params=pltpu.CompilerParams(
            collective_id=0, has_side_effects=True, vmem_limit_bytes=40 << 20
        ),
    )(*[pltpu.with_memory_space_constraint(a, pltpu.HBM) for a in (tokens, upstream, weight_a, weight_b)])
    return pl.pallas_call(
        copy_kernel,
        out_shape=results,
        in_specs=[anywhere] * 4 + [pl.BlockSpec(memory_space=pltpu.VMEM)] * 2,
        out_specs=[anywhere] * 4,
        scratch_shapes=[pltpu.VMEM((rows, size), BF16), dma((5,))],
    )(*[pltpu.with_memory_space_constraint(a, pltpu.VMEM) for a in made])


def copy_kernel(out, gi, ga, gb, own, last, out_to, gi_to, ga_to, gb_to, block, sems):
    done = gi.shape[1]
    copies = [
        pltpu.make_async_copy(out, out_to, sems.at[0]),
        pltpu.make_async_copy(gi, gi_to.at[:, pl.ds(0, done)], sems.at[1]),
        pltpu.make_async_copy(ga, ga_to, sems.at[2]),
        pltpu.make_async_copy(gb, gb_to, sems.at[3]),
        pltpu.make_async_copy(block, gi_to.at[:, pl.ds(done, block.shape[1])], sems.at[4]),
    ]
    for c in copies[:4]:
        c.start()
    block[...] = (own[...] + last[...].astype(F32)).astype(BF16)
    copies[4].start()
    for c in copies:
        c.wait()


def solution(mesh):
    in_specs = (
        P("dp", "bfly"),
        P(None, "bfly", None, None),
        P(None, "bfly", None, None),
        P("dp", "bfly"),
    )
    out_specs = (
        P("dp", "bfly"),
        P("dp", "bfly"),
        P("dp", None, "bfly", None),
        P("dp", None, "bfly", None),
    )
    return jax.shard_map(
        functools.partial(shards, mesh.shape["dp"]),
        mesh=mesh,
        in_specs=in_specs,
        out_specs=out_specs,
        check_vma=False,
    )
```
